256 devices in a mesh: ctx: 256 (over z, x, y, core).
Axes of the slice: x: 4, y: 4, z: 8, core: 2. Of those that a mesh axis runs over, the one named last changes fastest.
Arguments:
- queries: bfloat16 [65536, 2048], P('ctx'), may hold values from -6 to 6
- key_rows: bfloat16 [65536, 2048], P('ctx'), may hold values from -6 to 6
- value_rows: bfloat16 [65536, 2048], P('ctx'), may hold values from -6 to 6
- token_rates: float32 [65536], P('ctx'), may hold values from 0.0001953125 to 0.001953125
- fast_weights: bfloat16 [4, 3, 512, 512], replicated, may hold values from -0.25 to 0.25
- out_gain: float32 [4, 512], replicated, may hold values from 0.1 to 0.4
- proj_weight: bfloat16 [2048, 2048], P(None, 'ctx'), may hold values from -0.125 to 0.125
Outputs:
- layer_out: bfloat16 [65536, 2048], P('ctx')
The draws below stay inside these ranges and needn't reach their ends.
All inputs are finite; a program needn't handle non-finite values.
Results may differ from the reference program's by a relative error of at most 0.013.
Values may be sent and summed in bfloat16 or wider, within the bound.
A program may use at most 128 MiB of HBM per device.

```python
import math
import jax
import jax.numpy as jnp
from jax import lax

HEADS = 4
HD = 512
D = 2048
TOK_DEV = 256
WINDOW = 256
TOKENS = 65536


def draw_queries(key, part):
    key = jax.random.fold_in(key, 11)
    base = jnp.clip(jax.random.normal(key, (TOKENS, D), jnp.float32), -6.0, 6.0)
    return base.astype(jnp.bfloat16)


def draw_key_rows(key, part):
    key = jax.random.fold_in(key, 23)
    base = jnp.clip(jax.random.normal(key, (TOKENS, D), jnp.float32), -6.0, 6.0)
    return base.astype(jnp.bfloat16)


def block_scale(stream_key, shape, cuts, smallest, largest):
    factor_of, own = 1.0, jax.random.fold_in(stream_key, 6)
    for position, parts in cuts:
        heights = jnp.exp(jax.random.uniform(jax.random.fold_in(own, position), (parts,), jnp.float32, smallest / len(cuts), largest / len(cuts)))
        factor_of = factor_of * jnp.repeat(heights, shape[position] // parts).reshape([-1 if axis == position else 1 for axis in range(len(shape))])
    return factor_of


def bell_draw(stream_key, dims, width, bound, cuts=(), kind=jnp.bfloat16):
    level = block_scale(stream_key, dims, cuts, -0.22, 0.18) if cuts else 1.0
    result = jax.random.normal(stream_key, dims, jnp.float32) * width * level
    return jnp.minimum(jnp.maximum(result, -bound), bound).astype(kind)


def setup_inputs(seed: int = 0) -> dict:
    seeds = jax.random.split(jax.random.key(seed), 8)
    queries = draw_queries(jax.random.fold_in(seeds[7], 71), 0)
    key_rows = draw_key_rows(jax.random.fold_in(seeds[7], 71), 0)
    value_rows = bell_draw(seeds[2], (TOKENS, D), 1.0, 6.0, ((0, 256),))
    token_rates = jnp.clip(jnp.exp(math.log(0.001953125) - 2.3025851 * jax.random.uniform(seeds[3], (TOKENS,), jnp.float32) ** block_scale(seeds[3], (TOKENS,), ((0, 256),), -0.2, 0.2)), 0.0001953125, 0.001953125)
    fast_weights = bell_draw(seeds[4], (HEADS, 3, HD, HD), HD ** -0.5, 0.25)
    out_gain = jnp.clip(jax.random.uniform(seeds[5], (HEADS, HD), jnp.float32, 0.1, 0.4), 0.1, 0.4)
    proj_weight = bell_draw(seeds[6], (D, D), D ** -0.5, 0.125, ((1, 256),))
    return dict(queries=queries, key_rows=key_rows, value_rows=value_rows, token_rates=token_rates, fast_weights=fast_weights, out_gain=out_gain, proj_weight=proj_weight)


epsilon = 1e-06

def renorm_rows(weights, grads):
    shifted = weights - grads
    target = jnp.sqrt(lax.optimization_barrier(jnp.mean(weights * weights, axis=-1, keepdims=True)) + epsilon)
    current = jnp.sqrt(lax.optimization_barrier(jnp.mean(shifted * shifted, axis=-1, keepdims=True)) + epsilon)
    return shifted * (target / current)

def head_grads(keys, values, token_rates, weights_bf):
    pre_gate = jnp.dot(keys, weights_bf[0], preferred_element_type=jnp.float32)
    pre_up = jnp.dot(keys, weights_bf[2], preferred_element_type=jnp.float32)
    gate_sig = jax.nn.sigmoid(pre_gate)
    hidden = (pre_gate * gate_sig * pre_up).astype(jnp.bfloat16)
    out_grad = (-token_rates[:, None] * values.astype(jnp.float32)).astype(jnp.bfloat16)
    grad_down = jnp.dot(hidden.T, out_grad, preferred_element_type=jnp.float32)
    hidden_grad = jnp.dot(out_grad, weights_bf[1].T, preferred_element_type=jnp.float32)
    gate_grad = (hidden_grad * pre_up * gate_sig * (1.0 + pre_gate * (1.0 - gate_sig))).astype(jnp.bfloat16)
    up_grad = (hidden_grad * pre_gate * gate_sig).astype(jnp.bfloat16)
    grad_gate = jnp.dot(keys.T, gate_grad, preferred_element_type=jnp.float32)
    grad_up = jnp.dot(keys.T, up_grad, preferred_element_type=jnp.float32)
    return jnp.stack([grad_gate, grad_down, grad_up])

def head_forward(query_part, updated, gain):
    query_gate = jnp.dot(query_part, updated[0], preferred_element_type=jnp.float32)
    query_up = jnp.dot(query_part, updated[2], preferred_element_type=jnp.float32)
    fast_hidden = (jax.nn.silu(query_gate) * query_up).astype(jnp.bfloat16)
    fast_out = jnp.dot(fast_hidden, updated[1], preferred_element_type=jnp.float32)
    return fast_out * lax.rsqrt(lax.optimization_barrier(jnp.mean(fast_out * fast_out, axis=-1, keepdims=True)) + epsilon) * gain

def head_attend(query_part, keys, values):
    block_rows = min(512, TOK_DEV)
    blocks_count = TOKENS // block_rows
    key_padded = jnp.concatenate([jnp.zeros((WINDOW, HD), jnp.bfloat16), keys], axis=0)
    value_padded = jnp.concatenate([jnp.zeros((WINDOW, HD), jnp.bfloat16), values], axis=0)
    score_scale = HD ** (-0.5)
    row_pos = lax.broadcasted_iota(jnp.int32, (block_rows, block_rows + WINDOW), 0)
    col_pos = lax.broadcasted_iota(jnp.int32, (block_rows, block_rows + WINDOW), 1)

    def one_block(block_index):
        first = (block_index * block_rows).astype(jnp.int32)
        query_block = lax.dynamic_slice_in_dim(query_part, first, block_rows, 0)
        key_block = lax.dynamic_slice_in_dim(key_padded, first, block_rows + WINDOW, 0)
        value_block = lax.dynamic_slice_in_dim(value_padded, first, block_rows + WINDOW, 0)
        scores = jnp.dot(query_block, key_block.T, preferred_element_type=jnp.float32) * score_scale
        valid = (col_pos > row_pos) & (col_pos <= row_pos + WINDOW) & (first + col_pos - WINDOW >= 0)
        scores = jnp.where(valid, scores, -1e+30)
        top = lax.optimization_barrier(jnp.max(scores, axis=-1, keepdims=True))
        expd = jnp.where(valid, jnp.exp(scores - top), 0.0)
        prob_rows = (expd / lax.optimization_barrier(jnp.sum(expd, axis=-1, keepdims=True))).astype(jnp.bfloat16)
        return jnp.dot(prob_rows, value_block, preferred_element_type=jnp.float32)
    return lax.map(one_block, jnp.arange(blocks_count, dtype=jnp.int32)).reshape(TOKENS, HD)

def reference(queries, key_rows, value_rows, token_rates, fast_weights, out_gain, proj_weight):
    grads = []
    for head in range(HEADS):
        cols = slice(head * HD, (head + 1) * HD)
        grads.append(head_grads(key_rows[:, cols], value_rows[:, cols], token_rates, fast_weights[head]))
    stacked = jnp.stack(grads)
    updated = renorm_rows(fast_weights.astype(jnp.float32), stacked).astype(jnp.bfloat16)
    pieces = []
    for head in range(HEADS):
        cols = slice(head * HD, (head + 1) * HD)
        normed = head_forward(queries[:, cols], updated[head], out_gain[head])
        attended = head_attend(queries[:, cols], key_rows[:, cols], value_rows[:, cols])
        pieces.append((attended + normed).astype(jnp.bfloat16))
    combined = jnp.concatenate(pieces, axis=1)
    return jnp.dot(combined, proj_weight, preferred_element_type=jnp.float32).astype(jnp.bfloat16)
```

```python
import functools

import jax
import jax.numpy as jnp
from jax import lax
from jax.experimental import pallas as pl
from jax.experimental.pallas import tpu as pltpu
from jax.sharding import PartitionSpec as P

HD = 512
TOK = 256
EPS = 1e-06
F32 = jnp.float32
BF16 = jnp.bfloat16
MESH = pl.DeviceIdType.MESH


def mm(a, b):
    return jnp.dot(a, b, preferred_element_type=F32)


def mm_nt(a, b):
    return lax.dot_general(a, b, (((1,), (1,)), ((), ())), preferred_element_type=F32)


def mm_tn(a, b):
    return lax.dot_general(a, b, (((0,), (0,)), ((), ())), preferred_element_type=F32)


def aligned(index, step):
    return pl.multiple_of(index * step, step)


def kernel(
    q_hbm, k_hbm, v_hbm, rates_ref, w_hbm, gain_ref, proj_ref, out_hbm,
    qb, kb, vb, wb, rates_st, rates_sib, pst, prx, pj,
    pg, pu, hg, og, hid, gg, ug,
    gb, ra, rb, fl, fr, sec, rsec, zacc, w32, zs, rz, agz, wn,
    att, comb, osend, orecv, obuf,
    loc_sem, sib_send, sib_recv, prim_send, prim_recv, sec_send, sec_recv,
    z_send, z_recv, agz_send, agz_recv, agsec_send, agsec_recv, agp_send, agp_recv,
    py_send, py_recv, px_send, px_recv, pz_send, pz_recv, halo_send, halo_recv,
    os_send, os_recv, out_sem,
):
    me = lax.axis_index("ctx")
    core = lax.rem(me, 2)
    chip = lax.div(me, 2)
    y = lax.rem(chip, 4)
    x = lax.rem(lax.div(chip, 4), 4)
    z = lax.div(chip, 16)
    sib = me + 1 - 2 * core
    p = core * y + (1 - core) * x
    s = core * x + (1 - core) * y
    p_step = 8 - 6 * core
    s_step = 2 + 6 * core

    def along(position, size, step, by):
        return me + (lax.rem(position + by, size) - position) * step

    right = along(p, 4, p_step, 1)
    left = along(p, 4, p_step, 3)
    z_right = along(z, 8, 32, 1)
    z_left = along(z, 8, 32, 7)
    nxt = lax.rem(me + 2, 256)
    prv = lax.rem(me + 254, 256)

    def remote(src, dst, send, recv, device):
        return pltpu.make_async_remote_copy(
            src_ref=src, dst_ref=dst, send_sem=send, recv_sem=recv,
            device_id=(device,), device_id_type=MESH,
        )

    pending = []

    def go(copies):
        for copy in copies:
            copy.start()
            pending.append(copy)
        return copies

    mine = pl.ds(aligned(core, 1024), 1024)
    theirs = pl.ds(aligned(1 - core, 1024), 1024)
    my_rows = aligned(core, TOK)
    locals_ = [
        pltpu.make_async_copy(k_hbm.at[:, mine], kb.at[pl.ds(256 + my_rows, TOK), :], loc_sem.at[0]),
        pltpu.make_async_copy(w_hbm.at[pl.ds(2 * core, 2)], wb, loc_sem.at[1]),
        pltpu.make_async_copy(v_hbm.at[:, mine], vb.at[pl.ds(256 + my_rows, TOK), :], loc_sem.at[2]),
        pltpu.make_async_copy(q_hbm.at[:, mine], qb.at[pl.ds(my_rows, TOK), :], loc_sem.at[3]),
    ]
    for copy in locals_:
        copy.start()

    barrier = pltpu.get_barrier_semaphore()
    partners = [sib, nxt, prv]
    partners += [along(x, 4, 8, d) for d in (1, 2, 3)]
    partners += [along(y, 4, 2, d) for d in (1, 2, 3)]
    partners += [along(z, 8, 32, d) for d in range(1, 8)]
    for device in partners:
        pl.semaphore_signal(barrier, inc=1, device_id=(device,), device_id_type=MESH)

    rates_st[0:2, :] = rates_ref[...]
    rates_st[2:8, :] = jnp.zeros((6, 128), F32)
    shard = proj_ref[...].astype(F32)
    first_core = core == 0
    own_half = jnp.where(first_core, shard[:, :1024], shard[:, 1024:])
    sib_half = jnp.where(first_core, shard[:, 1024:], shard[:, :1024])
    pst[...] = jnp.concatenate([sib_half, sib_half], axis=0).astype(BF16)

    pl.semaphore_wait(barrier, len(partners))

    to_sib = [
        (pst, prx),
        (rates_st, rates_sib),
        (k_hbm.at[:, theirs], kb.at[pl.ds(256 + my_rows, TOK), :]),
        (v_hbm.at[:, theirs], vb.at[pl.ds(256 + my_rows, TOK), :]),
        (q_hbm.at[:, theirs], qb.at[pl.ds(my_rows, TOK), :]),
    ]
    sib_copies = go([
        remote(src, dst, sib_send.at[i], sib_recv.at[i], sib)
        for i, (src, dst) in enumerate(to_sib)
    ])

    def grads_rows(j, block, rates):
        cols = slice(j * HD, (j + 1) * HD)
        rows = aligned(block, TOK)
        keys = kb[pl.ds(256 + rows, TOK), cols]
        for i in range(2):
            rate = jnp.transpose(jnp.broadcast_to(rates[i:i + 1, :], (128, 128)))
            rate = jnp.concatenate([rate] * 4, axis=1)
            values = vb[pl.ds(256 + rows + i * 128, 128), cols].astype(F32)
            og[j, pl.ds(rows + i * 128, 128), :] = (-rate * values).astype(BF16)
        pg[...] = mm(keys, wb[j, 0])
        pu[...] = mm(keys, wb[j, 2])
        hg[...] = mm_nt(og[j, pl.ds(rows, TOK), :], wb[j, 1])

        def step(i, carry):
            part = pl.ds(aligned(i, 32), 32)
            dest = pl.ds(rows + aligned(i, 32), 32)
            gate, up, grad = pg[part, :], pu[part, :], hg[part, :]
            sig = jax.nn.sigmoid(gate)
            act = gate * sig
            hid[j, dest, :] = (act * up).astype(BF16)
            gg[j, dest, :] = (grad * up * sig * (1.0 + gate * (1.0 - sig))).astype(BF16)
            ug[j, dest, :] = (grad * act).astype(BF16)
            return carry

        lax.fori_loop(0, 8, step, 0)

    def grads_sum(j):
        def step(i, carry):
            lanes = pl.ds(pl.multiple_of(j * HD + i * 256, 256), 256)
            out = pl.ds(aligned(i, 256), 256)
            keys = kb[256:768, lanes]
            gb[3 * j, out, :] = mm_tn(keys, gg[j]).astype(BF16)
            gb[3 * j + 2, out, :] = mm_tn(keys, ug[j]).astype(BF16)
            gb[3 * j + 1, out, :] = mm_tn(hid[j, :, pl.ds(aligned(i, 256), 256)], og[j]).astype(BF16)
            return carry

        lax.fori_loop(0, 2, step, 0)

    def chunk_rows(by, part):
        start = lax.rem(p + by, 4) * 128 + part * 64
        return pl.ds(pl.multiple_of(start, 64), 64)

    def prim_first(j):
        mats = pl.ds(3 * j, 3)
        moves = [
            (gb.at[mats, chunk_rows(2, 0), :], ra.at[mats], right),
            (gb.at[mats, chunk_rows(2, 1), :], rb.at[mats], left),
            (gb.at[mats, chunk_rows(1, 1), :], fl.at[mats, 64:128, :], right),
            (gb.at[mats, chunk_rows(3, 0), :], fr.at[mats, 0:64, :], left),
        ]
        return go([
            remote(src, dst, prim_send.at[6 * j + i], prim_recv.at[6 * j + i], dev)
            for i, (src, dst, dev) in enumerate(moves)
        ])

    def add_into(j, rows, extra):
        for m in range(3 * j, 3 * j + 3):
            total = gb[m, rows, :].astype(F32) + extra[m].astype(F32)
            gb[m, rows, :] = total.astype(BF16)

    def prim_second(j, first):
        mats = pl.ds(3 * j, 3)
        first[0].wait_recv()
        add_into(j, chunk_rows(1, 0), ra)
        a = remote(gb.at[mats, chunk_rows(1, 0), :], fl.at[mats, 0:64, :],
                   prim_send.at[6 * j + 4], prim_recv.at[6 * j + 4], right)
        go([a])
        first[1].wait_recv()
        add_into(j, chunk_rows(3, 1), rb)
        b = remote(gb.at[mats, chunk_rows(3, 1), :], fr.at[mats, 64:128, :],
                   prim_send.at[6 * j + 5], prim_recv.at[6 * j + 5], left)
        go([b])
        return [first[2], first[3], a, b]

    def prim_last(j, copies):
        for copy in copies:
            copy.wait_recv()

        def step(i, carry):
            rows = pl.ds(aligned(i, 32), 32)
            own = pl.ds(pl.multiple_of(p * 128 + i * 32, 32), 32)
            for m in range(3 * j, 3 * j + 3):
                total = gb[m, own, :].astype(F32) + fl[m, rows, :].astype(F32)
                sec[m, rows, :] = (total + fr[m, rows, :].astype(F32)).astype(BF16)
            return carry

        lax.fori_loop(0, 4, step, 0)

    def sec_sends(j):
        mats = pl.ds(3 * j, 3)
        out = []
        for d in (1, 2, 3):
            rows = pl.ds(aligned(lax.rem(s + d, 4), 32), 32)
            out.append(remote(sec.at[mats, rows, :], rsec.at[d - 1, mats],
                              sec_send.at[3 * j + d - 1], sec_recv.at[3 * j + d - 1],
                              along(s, 4, s_step, d)))
        return go(out)

    def sec_last(j, copies):
        for copy in copies:
            copy.wait_recv()
        own = pl.ds(aligned(s, 32), 32)
        for m in range(3 * j, 3 * j + 3):
            total = sec[m, own, :].astype(F32)
            for d in range(3):
                total = total + rsec[d, m].astype(F32)
            zacc[32 * m:32 * m + 32, :] = total

    def z_sends():
        for owner in range(8):
            for i in range(3):
                rows = slice(24 * owner + 8 * i, 24 * owner + 8 * i + 8)
                both = jnp.concatenate([zacc[rows, 0:256], zacc[rows, 256:512]], axis=0)
                zs[owner, :, i * 256:(i + 1) * 256] = both.astype(BF16)
        return go([
            remote(zs.at[lax.rem(z + d, 8)], rz.at[d - 1], z_send.at[d - 1], z_recv.at[d - 1],
                   along(z, 8, 32, d))
            for d in range(1, 8)
        ])

    def renorm(copies):
        for copy in copies:
            copy.wait_recv()
        for i in range(3):
            lanes = slice(i * 256, (i + 1) * 256)
            total = rz[0, :, lanes].astype(F32)
            for d in range(1, 7):
                total = total + rz[d, :, lanes].astype(F32)
            rows = pl.ds(pl.multiple_of(24 * z + 8 * i, 8), 8)
            grad = zacc[rows, :] + jnp.concatenate([total[0:8], total[8:16]], axis=1)
            weights = w32[rows, :]
            shifted = weights - grad
            target = jnp.sqrt(jnp.mean(weights * weights, axis=-1, keepdims=True) + EPS)
            current = jnp.sqrt(jnp.mean(shifted * shifted, axis=-1, keepdims=True) + EPS)
            fresh = shifted * (target / current)
            both = jnp.concatenate([fresh[:, 0:256], fresh[:, 256:512]], axis=0)
            agz[z, :, lanes] = both.astype(BF16)
        return go([
            remote(agz.at[z], agz.at[z], agz_send.at[d - 1], agz_recv.at[d - 1],
                   along(z, 8, 32, d))
            for d in range(1, 8)
        ])

    own_block = pl.ds(pl.multiple_of(128 * p + 32 * s, 32), 32)

    def unpack(copies):
        for copy in copies:
            copy.wait_recv()
        for m in range(6):
            groups = []
            for g in range(4 * m, 4 * m + 4):
                both = agz[g // 3, :, (g % 3) * 256:(g % 3 + 1) * 256].astype(F32)
                groups.append(jnp.concatenate([both[0:8], both[8:16]], axis=1))
            wn[m, own_block, :] = jnp.concatenate(groups, axis=0).astype(BF16)

    def agsec_sends(j):
        part = wn.at[pl.ds(3 * j, 3), own_block, :]
        return go([
            remote(part, part, agsec_send.at[3 * j + d - 1], agsec_recv.at[3 * j + d - 1],
                   along(s, 4, s_step, d))
            for d in (1, 2, 3)
        ])

    def agp_first(j):
        mats = pl.ds(3 * j, 3)
        half_a = wn.at[mats, chunk_rows(0, 0), :]
        half_b = wn.at[mats, chunk_rows(0, 1), :]
        moves = [(half_a, right), (half_b, left), (half_b, right), (half_a, left)]
        return go([
            remote(ref, ref, agp_send.at[6 * j + i], agp_recv.at[6 * j + i], dev)
            for i, (ref, dev) in enumerate(moves)
        ])

    def agp_second(j, first):
        mats = pl.ds(3 * j, 3)
        first[0].wait_recv()
        half_a = wn.at[mats, chunk_rows(3, 0), :]
        a = remote(half_a, half_a, agp_send.at[6 * j + 4], agp_recv.at[6 * j + 4], right)
        go([a])
        first[1].wait_recv()
        half_b = wn.at[mats, chunk_rows(1, 1), :]
        b = remote(half_b, half_b, agp_send.at[6 * j + 5], agp_recv.at[6 * j + 5], left)
        go([b])
        return [first[2], first[3], a, b]

    def attend(j, block):
        cols = slice(j * HD, (j + 1) * HD)
        first = block * TOK
        pg[...] = mm_nt(qb[first:first + TOK, cols], kb[first:first + 2 * TOK, cols])

        def step(i, carry):
            part = pl.ds(aligned(i, 32), 32)
            row = lax.broadcasted_iota(jnp.int32, (32, 512), 0) + i * 32
            col = lax.broadcasted_iota(jnp.int32, (32, 512), 1)
            valid = (col > row) & (col <= row + 256)
            if block == 0:
                valid = valid & (chip * 512 + col >= 256)
            scores = jnp.where(valid, pg[part, :] * (HD ** -0.5), -1e30)
            top = jnp.max(scores, axis=-1, keepdims=True)
            expd = jnp.exp(scores - top)
            probs = expd / jnp.sum(expd, axis=-1, keepdims=True)
            gg[0, part, :] = probs.astype(BF16)
            return carry

        lax.fori_loop(0, 8, step, 0)
        att[first:first + TOK, cols] = mm(gg[0, 0:TOK, :], vb[first:first + 2 * TOK, cols])

    def forward(j):
        cols = slice(j * HD, (j + 1) * HD)
        gain = gain_ref[pl.ds(2 * core + j, 1), :]

        def block(b, carry):
            rows = aligned(b, TOK)
            queries = qb[pl.ds(rows, TOK), cols]
            pg[...] = mm(queries, wn[3 * j])
            pu[...] = mm(queries, wn[3 * j + 2])

            def act(i, inner):
                part = pl.ds(aligned(i, 32), 32)
                gate = pg[part, :]
                gg[0, part, :] = (gate * jax.nn.sigmoid(gate) * pu[part, :]).astype(BF16)
                return inner

            lax.fori_loop(0, 8, act, 0)
            hg[...] = mm(gg[0, 0:TOK, :], wn[3 * j + 1])

            def norm(i, inner):
                part = pl.ds(aligned(i, 32), 32)
                dest = pl.ds(rows + aligned(i, 32), 32)
                fast = hg[part, :]
                scale = lax.rsqrt(jnp.mean(fast * fast, axis=-1, keepdims=True) + EPS)
                comb[dest, cols] = (att[dest, cols] + fast * scale * gain).astype(BF16)
                return inner

            lax.fori_loop(0, 8, norm, 0)
            return carry

        lax.fori_loop(0, 2, block, 0)

    for copy in locals_[:3]:
        copy.wait()
    for j in range(2):
        grads_rows(j, core, rates_ref[...])

    sib_copies[0].wait_recv()
    received = prx[...].astype(F32)[0:8]
    pair = jnp.concatenate(
        [jnp.where(first_core, own_half, received), jnp.where(first_core, received, own_half)], axis=0
    )
    pj[pl.ds(aligned(chip, 16), 16), :] = pair.astype(BF16)
    part = pj.at[pl.ds(aligned(chip, 16), 16), :]
    py = go([
        remote(part, part, py_send.at[d - 1], py_recv.at[d - 1], along(y, 4, 2, d))
        for d in (1, 2, 3)
    ])

    for copy in sib_copies[1:4]:
        copy.wait_recv()
    grads_rows(0, 1 - core, rates_sib[...])
    grads_sum(0)
    prim0 = prim_first(0)

    for copy in py:
        copy.wait_recv()
    part = pj.at[pl.ds(aligned(lax.div(chip, 4), 64), 64), :]
    px = go([
        remote(part, part, px_send.at[d - 1], px_recv.at[d - 1], along(x, 4, 8, d))
        for d in (1, 2, 3)
    ])

    grads_rows(1, 1 - core, rates_sib[...])
    grads_sum(1)
    prim1 = prim_first(1)
    prim0 = prim_second(0, prim0)

    def plane(by, lo=0, size=256):
        start = lax.rem(z + by, 8) * 256 + lo
        return pj.at[pl.ds(pl.multiple_of(start, 128), size), :]

    def pz(step, by_right, by_left, lo_right=0, lo_left=0, size=256):
        a = plane(by_right, lo_right, size)
        b = plane(by_left, lo_left, size)
        return go([
            remote(a, a, pz_send.at[2 * step], pz_recv.at[2 * step], z_right),
            remote(b, b, pz_send.at[2 * step + 1], pz_recv.at[2 * step + 1], z_left),
        ])

    for copy in px:
        copy.wait_recv()
    pz0 = pz(0, 0, 0)

    locals_[3].wait()
    sib_copies[4].wait_recv()
    attend(0, 1)
    prim1 = prim_second(1, prim1)
    prim_last(0, prim0)
    sec0 = sec_sends(0)

    for m in range(6):
        w32[32 * m:32 * m + 32, :] = wb[m // 3, m % 3, own_block, :].astype(F32)
    attend(1, 1)

    prim_last(1, prim1)
    sec1 = sec_sends(1)
    halo = go([
        remote(buf.at[512:768, :], buf.at[0:256, :], halo_send.at[i], halo_recv.at[i], nxt)
        for i, buf in enumerate((kb, vb))
    ])
    sec_last(0, sec0)
    sec_last(1, sec1)
    zc = z_sends()
    for copy in pz0:
        copy.wait_recv()
    pz1 = pz(1, 7, 1)
    ag = renorm(zc)
    unpack(ag)
    ags0 = agsec_sends(0)
    ags1 = agsec_sends(1)
    for copy in ags0:
        copy.wait_recv()
    agp0 = agp_first(0)
    for copy in ags1:
        copy.wait_recv()
    agp1 = agp_first(1)
    for copy in halo:
        copy.wait_recv()
    attend(0, 0)
    agp0 = agp_second(0, agp0)
    for copy in pz1:
        copy.wait_recv()
    pz2 = pz(2, 6, 2)
    attend(1, 0)
    agp1 = agp_second(1, agp1)
    for copy in agp0:
        copy.wait_recv()
    forward(0)
    for copy in pz2:
        copy.wait_recv()
    pz3 = pz(3, 5, 3, 0, 128, 128)
    for copy in agp1:
        copy.wait_recv()
    forward(1)
    for copy in pz3:
        copy.wait_recv()

    def partial(rows, n):
        return mm_nt(comb[pl.ds(rows, TOK), :], pj[pl.ds(n * 512, 512), :])

    outs = []
    for n in range(4):
        osend[n] = partial(aligned(1 - core, TOK), n).astype(BF16)
        outs += go([remote(osend.at[n], orecv.at[n], os_send.at[n], os_recv.at[n], sib)])
    finals = []
    for n in range(4):
        total = partial(my_rows, n)
        outs[n].wait_recv()
        obuf[n] = (total + orecv[n].astype(F32)).astype(BF16)
        copy = pltpu.make_async_copy(obuf.at[n], out_hbm.at[:, n * 512:(n + 1) * 512], out_sem.at[n])
        copy.start()
        finals.append(copy)
    for copy in pending:
        copy.wait_send()
    for copy in finals:
        copy.wait()


def body(queries, key_rows, value_rows, token_rates, fast_weights, out_gain, proj_weight):
    anywhere = pl.BlockSpec(memory_space=pl.ANY)
    vmem = pl.BlockSpec(memory_space=pltpu.VMEM)
    sem = pltpu.SemaphoreType.DMA
    scratch = [
        pltpu.VMEM((512, 1024), BF16),
        pltpu.VMEM((768, 1024), BF16),
        pltpu.VMEM((768, 1024), BF16),
        pltpu.VMEM((2, 3, 512, 512), BF16),
        pltpu.VMEM((8, 128), F32),
        pltpu.VMEM((8, 128), F32),
        pltpu.VMEM((16, 1024), BF16),
        pltpu.VMEM((16, 1024), BF16),
        pltpu.VMEM((2048, 1024), BF16),
        pltpu.VMEM((256, 512), F32),
        pltpu.VMEM((256, 512), F32),
        pltpu.VMEM((256, 512), F32),
        pltpu.VMEM((2, 512, 512), BF16),
        pltpu.VMEM((2, 512, 512), BF16),
        pltpu.VMEM((2, 512, 512), BF16),
        pltpu.VMEM((2, 512, 512), BF16),
        pltpu.VMEM((6, 512, 512), BF16),
        pltpu.VMEM((6, 64, 512), BF16),
        pltpu.VMEM((6, 64, 512), BF16),
        pltpu.VMEM((6, 128, 512), BF16),
        pltpu.VMEM((6, 128, 512), BF16),
        pltpu.VMEM((6, 128, 512), BF16),
        pltpu.VMEM((3, 6, 32, 512), BF16),
        pltpu.VMEM((192, 512), F32),
        pltpu.VMEM((192, 512), F32),
        pltpu.VMEM((8, 16, 768), BF16),
        pltpu.VMEM((7, 16, 768), BF16),
        pltpu.VMEM((8, 16, 768), BF16),
        pltpu.VMEM((6, 512, 512), BF16),
        pltpu.VMEM((512, 1024), F32),
        pltpu.VMEM((512, 1024), BF16),
        pltpu.VMEM((4, 256, 512), BF16),
        pltpu.VMEM((4, 256, 512), BF16),
        pltpu.VMEM((4, 256, 512), BF16),
        sem((4,)),
        sem((5,)), sem((5,)),
        sem((12,)), sem((12,)),
        sem((6,)), sem((6,)),
        sem((7,)), sem((7,)),
        sem((7,)), sem((7,)),
        sem((6,)), sem((6,)),
        sem((12,)), sem((12,)),
        sem((3,)), sem((3,)),
        sem((3,)), sem((3,)),
        sem((8,)), sem((8,)),
        sem((2,)), sem((2,)),
        sem((4,)), sem((4,)),
        sem((4,)),
    ]
    return pl.pallas_call(
        kernel,
        out_shape=jax.ShapeDtypeStruct((TOK, 2048), BF16),
        in_specs=[anywhere, anywhere, anywhere, vmem, anywhere, vmem, vmem],
        out_specs=anywhere,
        scratch_shapes=scratch,
        compiler_params=pltpu.CompilerParams(
            collective_id=0, has_side_effects=True, vmem_limit_bytes=56 * 1024 * 1024
        ),
        cost_estimate=pl.CostEstimate(flops=12 * 10**9, bytes_accessed=10**7, transcendentals=10**6),
    )(
        queries, key_rows, value_rows, token_rates.reshape(2, 128), fast_weights, out_gain,
        proj_weight.T,
    )


def solution(mesh):
    return jax.shard_map(
        body,
        mesh=mesh,
        in_specs=(
            P("ctx", None),
            P("ctx", None),
            P("ctx", None),
            P("ctx"),
            P(),
            P(),
            P(None, "ctx"),
        ),
        out_specs=P("ctx", None),
        check_vma=False,
    )
```

```python
import functools

import jax
import jax.numpy as jnp
from jax import lax
from jax.experimental import pallas as pl
from jax.experimental.pallas import tpu as pltpu
from jax.sharding import PartitionSpec as P

HD = 512
TOK = 256
EPS = 1e-06
CUT = 768
F32 = jnp.float32
BF16 = jnp.bfloat16
MESH = pl.DeviceIdType.MESH


def mm(a, b):
    return jnp.dot(a, b, preferred_element_type=F32)


def mm_nt(a, b):
    return lax.dot_general(a, b, (((1,), (1,)), ((), ())), preferred_element_type=F32)


def mm_tn(a, b):
    return lax.dot_general(a, b, (((0,), (0,)), ((), ())), preferred_element_type=F32)


def aligned(index, step):
    return pl.multiple_of(index * step, step)


def kernel(
    q_hbm, k_hbm, v_hbm, rates_ref, w_hbm, gain_ref, proj_ref, out_ref,
    qb, kb, vb, wb, rates_st, rates_sib, pst, prx, pj,
    pg, pu, hg, og, hid, gg, ug,
    gb, ra, rb, fl, fr, sec, rsec, zacc, wpk, zs, rz, agz, wn,
    att, comb, acc, osend, orecv,
    loc_sem, sib_send, sib_recv, prim_send, prim_recv, sec_send, sec_recv,
    z_send, z_recv, agz_send, agz_recv, agsec_send, agsec_recv, agp_send, agp_recv,
    py_send, py_recv, px_send, px_recv, pz_send, pz_recv,
    bz_send, bz_recv, by_send, by_recv, bx_send, bx_recv, halo_send, halo_recv,
    os_send, os_recv,
):
    me = lax.axis_index("ctx")
    core = lax.rem(me, 2)
    chip = lax.div(me, 2)
    y = lax.rem(chip, 4)
    x = lax.rem(lax.div(chip, 4), 4)
    z = lax.div(chip, 16)
    sib = me + 1 - 2 * core
    p = core * y + (1 - core) * x
    s = core * x + (1 - core) * y
    p_step = 8 - 6 * core
    s_step = 2 + 6 * core

    def along(position, size, step, by):
        return me + (lax.rem(position + by, size) - position) * step

    right = along(p, 4, p_step, 1)
    left = along(p, 4, p_step, 3)
    z_right = along(z, 8, 32, 1)
    z_left = along(z, 8, 32, 7)
    nxt = lax.rem(me + 2, 256)
    prv = lax.rem(me + 254, 256)

    def remote(src, dst, send, recv, device):
        return pltpu.make_async_remote_copy(
            src_ref=src, dst_ref=dst, send_sem=send, recv_sem=recv,
            device_id=(device,), device_id_type=MESH,
        )

    pending = []

    def go(copies):
        for copy in copies:
            copy.start()
            pending.append(copy)
        return copies

    mine = pl.ds(aligned(core, 1024), 1024)
    theirs = pl.ds(aligned(1 - core, 1024), 1024)
    my_rows = aligned(core, TOK)
    locals_ = [
        pltpu.make_async_copy(k_hbm.at[:, mine], kb.at[pl.ds(256 + my_rows, TOK), :], loc_sem.at[0]),
        pltpu.make_async_copy(w_hbm.at[pl.ds(2 * core, 2)], wb, loc_sem.at[1]),
        pltpu.make_async_copy(v_hbm.at[:, mine], vb.at[pl.ds(256 + my_rows, TOK), :], loc_sem.at[2]),
        pltpu.make_async_copy(q_hbm.at[:, mine], qb.at[pl.ds(my_rows, TOK), :], loc_sem.at[3]),
    ]
    for copy in locals_:
        copy.start()

    barrier = pltpu.get_barrier_semaphore()
    partners = [sib, nxt, prv]
    partners += [along(x, 4, 8, d) for d in (1, 2, 3)]
    partners += [along(y, 4, 2, d) for d in (1, 2, 3)]
    partners += [along(z, 8, 32, d) for d in range(1, 8)]
    for device in partners:
        pl.semaphore_signal(barrier, inc=1, device_id=(device,), device_id_type=MESH)

    rates_st[0:2, :] = rates_ref[...]
    rates_st[2:8, :] = jnp.zeros((6, 128), F32)
    shard = proj_ref[...].astype(F32)
    first_core = core == 0
    own_half = jnp.where(first_core, shard[:, :1024], shard[:, 1024:])
    sib_half = jnp.where(first_core, shard[:, 1024:], shard[:, :1024])
    pst[...] = jnp.concatenate([sib_half, sib_half], axis=0).astype(BF16)

    pl.semaphore_wait(barrier, len(partners))

    to_sib = [
        (pst, prx),
        (rates_st, rates_sib),
        (k_hbm.at[:, theirs], kb.at[pl.ds(256 + my_rows, TOK), :]),
        (v_hbm.at[:, theirs], vb.at[pl.ds(256 + my_rows, TOK), :]),
        (q_hbm.at[:, theirs], qb.at[pl.ds(my_rows, TOK), :]),
    ]
    sib_copies = go([
        remote(src, dst, sib_send.at[i], sib_recv.at[i], sib)
        for i, (src, dst) in enumerate(to_sib)
    ])

    def grads_rows(j, block, rates):
        cols = slice(j * HD, (j + 1) * HD)
        rows = aligned(block, TOK)
        keys = kb[pl.ds(256 + rows, TOK), cols]
        for i in range(2):
            rate = jnp.transpose(jnp.broadcast_to(rates[i:i + 1, :], (128, 128)))
            rate = jnp.concatenate([rate] * 4, axis=1)
            values = vb[pl.ds(256 + rows + i * 128, 128), cols].astype(F32)
            og[j, pl.ds(rows + i * 128, 128), :] = (-rate * values).astype(BF16)
        pg[...] = mm(keys, wb[j, 0])
        pu[...] = mm(keys, wb[j, 2])
        hg[...] = mm_nt(og[j, pl.ds(rows, TOK), :], wb[j, 1])

        def step(i, carry):
            part = pl.ds(aligned(i, 32), 32)
            dest = pl.ds(rows + aligned(i, 32), 32)
            gate, up, grad = pg[part, :], pu[part, :], hg[part, :]
            sig = jax.nn.sigmoid(gate)
            act = gate * sig
            hid[j, dest, :] = (act * up).astype(BF16)
            gg[j, dest, :] = (grad * up * sig * (1.0 + gate * (1.0 - sig))).astype(BF16)
            ug[j, dest, :] = (grad * act).astype(BF16)
            return carry

        lax.fori_loop(0, 8, step, 0)

    def grads_sum(j):
        def step(i, carry):
            lanes = pl.ds(pl.multiple_of(j * HD + i * 256, 256), 256)
            out = pl.ds(aligned(i, 256), 256)
            keys = kb[256:768, lanes]
            gb[3 * j, out, :] = mm_tn(keys, gg[j]).astype(BF16)
            gb[3 * j + 2, out, :] = mm_tn(keys, ug[j]).astype(BF16)
            gb[3 * j + 1, out, :] = mm_tn(hid[j, :, pl.ds(aligned(i, 256), 256)], og[j]).astype(BF16)
            return carry

        lax.fori_loop(0, 2, step, 0)

    def chunk_rows(by, part):
        start = lax.rem(p + by, 4) * 128 + part * 64
        return pl.ds(pl.multiple_of(start, 64), 64)

    def prim_first(j):
        mats = pl.ds(3 * j, 3)
        moves = [
            (gb.at[mats, chunk_rows(2, 0), :], ra.at[mats], right),
            (gb.at[mats, chunk_rows(2, 1), :], rb.at[mats], left),
            (gb.at[mats, chunk_rows(1, 1), :], fl.at[mats, 64:128, :], right),
            (gb.at[mats, chunk_rows(3, 0), :], fr.at[mats, 0:64, :], left),
        ]
        return go([
            remote(src, dst, prim_send.at[6 * j + i], prim_recv.at[6 * j + i], dev)
            for i, (src, dst, dev) in enumerate(moves)
        ])

    def add_into(j, rows, extra):
        for m in range(3 * j, 3 * j + 3):
            total = gb[m, rows, :].astype(F32) + extra[m].astype(F32)
            gb[m, rows, :] = total.astype(BF16)

    def prim_second(j, first):
        mats = pl.ds(3 * j, 3)
        first[0].wait_recv()
        add_into(j, chunk_rows(1, 0), ra)
        a = remote(gb.at[mats, chunk_rows(1, 0), :], fl.at[mats, 0:64, :],
                   prim_send.at[6 * j + 4], prim_recv.at[6 * j + 4], right)
        go([a])
        first[1].wait_recv()
        add_into(j, chunk_rows(3, 1), rb)
        b = remote(gb.at[mats, chunk_rows(3, 1), :], fr.at[mats, 64:128, :],
                   prim_send.at[6 * j + 5], prim_recv.at[6 * j + 5], left)
        go([b])
        return [first[2], first[3], a, b]

    def prim_last(j, copies):
        for copy in copies:
            copy.wait_recv()

        def step(i, carry):
            rows = pl.ds(aligned(i, 32), 32)
            own = pl.ds(pl.multiple_of(p * 128 + i * 32, 32), 32)
            for m in range(3 * j, 3 * j + 3):
                total = gb[m, own, :].astype(F32) + fl[m, rows, :].astype(F32)
                sec[m, rows, :] = (total + fr[m, rows, :].astype(F32)).astype(BF16)
            return carry

        lax.fori_loop(0, 4, step, 0)

    def sec_sends(j):
        mats = pl.ds(3 * j, 3)
        out = []
        for d in (1, 2, 3):
            rows = pl.ds(aligned(lax.rem(s + d, 4), 32), 32)
            out.append(remote(sec.at[mats, rows, :], rsec.at[d - 1, mats],
                              sec_send.at[3 * j + d - 1], sec_recv.at[3 * j + d - 1],
                              along(s, 4, s_step, d)))
        return go(out)

    def sec_last(j, copies):
        for copy in copies:
            copy.wait_recv()
        own = pl.ds(aligned(s, 32), 32)
        for m in range(3):
            total = sec[3 * j + m, own, :].astype(F32)
            for d in range(3):
                total = total + rsec[d, 3 * j + m].astype(F32)
            zacc[j, 32 * m:32 * m + 32, :] = total

    def pack(j, out):
        for group in range(24):
            rows = zacc[j, 4 * group:4 * group + 4, :]
            tall = jnp.concatenate([rows[:, c * 128:(c + 1) * 128] for c in range(4)], axis=0)
            lanes = slice(group % 3 * 128, (group % 3 + 1) * 128)
            out[j, group // 3, :, lanes] = tall.astype(BF16)

    def z_sends(j):
        pack(j, zs)
        return go([
            remote(zs.at[j, lax.rem(z + d, 8)], rz.at[j, d - 1],
                   z_send.at[7 * j + d - 1], z_recv.at[7 * j + d - 1], along(z, 8, 32, d))
            for d in range(1, 8)
        ])

    def renorm(j, copies):
        for copy in copies:
            copy.wait_recv()

        def rms(tall):
            square = tall * tall
            square = square[0:4] + square[4:8] + square[8:12] + square[12:16]
            return jnp.sqrt(jnp.sum(square, axis=-1, keepdims=True) * (1.0 / HD) + EPS)

        for i in range(3):
            lanes = slice(i * 128, (i + 1) * 128)
            grad = zs[j, z, :, lanes].astype(F32)
            for d in range(7):
                grad = grad + rz[j, d, :, lanes].astype(F32)
            weights = wpk[j, z, :, lanes].astype(F32)
            shifted = weights - grad
            scale = rms(weights) / rms(shifted)
            agz[j, z, :, lanes] = (shifted * jnp.concatenate([scale] * 4, axis=0)).astype(BF16)
        return go([
            remote(agz.at[j, z], agz.at[j, z], agz_send.at[7 * j + d - 1], agz_recv.at[7 * j + d - 1],
                   along(z, 8, 32, d))
            for d in range(1, 8)
        ])

    own_block = pl.ds(pl.multiple_of(128 * p + 32 * s, 32), 32)

    def unpack(j, copies):
        for copy in copies:
            copy.wait_recv()
        for m in range(3):
            rows = []
            for g in range(8 * m, 8 * m + 8):
                tall = agz[j, g // 3, :, g % 3 * 128:(g % 3 + 1) * 128].astype(F32)
                rows.append(jnp.concatenate([tall[4 * c:4 * c + 4] for c in range(4)], axis=1))
            wn[3 * j + m, own_block, :] = jnp.concatenate(rows, axis=0).astype(BF16)

    def agsec_sends(j):
        part = wn.at[pl.ds(3 * j, 3), own_block, :]
        return go([
            remote(part, part, agsec_send.at[3 * j + d - 1], agsec_recv.at[3 * j + d - 1],
                   along(s, 4, s_step, d))
            for d in (1, 2, 3)
        ])

    def agp_first(j):
        mats = pl.ds(3 * j, 3)
        half_a = wn.at[mats, chunk_rows(0, 0), :]
        half_b = wn.at[mats, chunk_rows(0, 1), :]
        moves = [(half_a, right), (half_b, left), (half_b, right), (half_a, left)]
        return go([
            remote(ref, ref, agp_send.at[6 * j + i], agp_recv.at[6 * j + i], dev)
            for i, (ref, dev) in enumerate(moves)
        ])

    def agp_second(j, first):
        mats = pl.ds(3 * j, 3)
        first[0].wait_recv()
        half_a = wn.at[mats, chunk_rows(3, 0), :]
        a = remote(half_a, half_a, agp_send.at[6 * j + 4], agp_recv.at[6 * j + 4], right)
        go([a])
        first[1].wait_recv()
        half_b = wn.at[mats, chunk_rows(1, 1), :]
        b = remote(half_b, half_b, agp_send.at[6 * j + 5], agp_recv.at[6 * j + 5], left)
        go([b])
        return [first[2], first[3], a, b]

    def attend(j, block):
        cols = slice(j * HD, (j + 1) * HD)
        first = block * TOK
        pg[...] = mm_nt(qb[first:first + TOK, cols], kb[first:first + 2 * TOK, cols])

        def step(i, carry):
            part = pl.ds(aligned(i, 64), 64)
            row = lax.broadcasted_iota(jnp.int32, (64, 512), 0) + i * 64
            col = lax.broadcasted_iota(jnp.int32, (64, 512), 1)
            valid = (col > row) & (col <= row + 256)
            if block == 0:
                valid = valid & (chip * 512 + col >= 256)
            scores = jnp.where(valid, pg[part, :] * (HD ** -0.5), -1e30)
            top = jnp.max(scores, axis=-1, keepdims=True)
            expd = jnp.exp(scores - top)
            probs = expd / jnp.sum(expd, axis=-1, keepdims=True)
            gg[0, part, :] = probs.astype(BF16)
            return carry

        lax.fori_loop(0, 4, step, 0)
        att[first:first + TOK, cols] = mm(gg[0, 0:TOK, :], vb[first:first + 2 * TOK, cols])

    def forward(j):
        cols = slice(j * HD, (j + 1) * HD)
        gain = gain_ref[pl.ds(2 * core + j, 1), :]

        def block(b, carry):
            rows = aligned(b, TOK)
            queries = qb[pl.ds(rows, TOK), cols]
            pg[...] = mm(queries, wn[3 * j])
            pu[...] = mm(queries, wn[3 * j + 2])

            def act(i, inner):
                part = pl.ds(aligned(i, 64), 64)
                gate = pg[part, :]
                gg[0, part, :] = (gate * jax.nn.sigmoid(gate) * pu[part, :]).astype(BF16)
                return inner

            lax.fori_loop(0, 4, act, 0)
            hg[...] = mm(gg[0, 0:TOK, :], wn[3 * j + 1])

            def norm(i, inner):
                part = pl.ds(aligned(i, 64), 64)
                dest = pl.ds(rows + aligned(i, 64), 64)
                fast = hg[part, :]
                scale = lax.rsqrt(jnp.mean(fast * fast, axis=-1, keepdims=True) + EPS)
                comb[dest, cols] = (att[dest, cols] + fast * scale * gain).astype(BF16)
                return inner

            lax.fori_loop(0, 4, norm, 0)
            return carry

        lax.fori_loop(0, 2, block, 0)

    for copy in locals_[:3]:
        copy.wait()
    for j in range(2):
        grads_rows(j, core, rates_ref[...])

    sib_copies[0].wait_recv()
    received = prx[...].astype(F32)[0:8]
    pair = jnp.concatenate(
        [jnp.where(first_core, own_half, received), jnp.where(first_core, received, own_half)], axis=0
    )
    lanes_a, lanes_b = slice(0, CUT), slice(CUT, 1024)
    spot = 4 * x + y
    place = pl.ds(aligned(spot, 16), 16)
    pj[z, place, :] = pair.astype(BF16)

    def same(ref, send, recv, device):
        return remote(ref, ref, send, recv, device)

    py = go([
        same(pj.at[z, place, lanes_a], py_send.at[d - 1], py_recv.at[d - 1], along(y, 4, 2, d))
        for d in (1, 2, 3)
    ])
    bz = go([
        same(pj.at[z, place, lanes_b], bz_send.at[d - 1], bz_recv.at[d - 1], along(z, 8, 32, d))
        for d in range(1, 8)
    ])

    def settle(copies):
        for copy in copies:
            copy.wait_recv()

    def pz(step, by_right, by_left, lo_right=0, lo_left=0, size=256):
        a = pj.at[lax.rem(z + by_right, 8), lo_right:lo_right + size, lanes_a]
        b = pj.at[lax.rem(z + by_left, 8), lo_left:lo_left + size, lanes_a]
        return go([
            same(a, pz_send.at[2 * step], pz_recv.at[2 * step], z_right),
            same(b, pz_send.at[2 * step + 1], pz_recv.at[2 * step + 1], z_left),
        ])

    x_right = along(x, 4, 8, 1)
    x_left = along(x, 4, 8, 3)

    def strip(by, half):
        start = lax.rem(x + by, 4) * 64 + half * 32
        return pj.at[:, pl.ds(pl.multiple_of(start, 32), 32), lanes_b]

    def bx(step, moves):
        return go([
            same(strip(by_, half), bx_send.at[4 * step + i], bx_recv.at[4 * step + i], dev)
            for i, (by_, half, dev) in enumerate(moves)
        ])

    def halo(i):
        buf, lanes = [(kb, slice(0, 512)), (kb, slice(512, 1024)), (vb, slice(0, 512)), (vb, slice(512, 1024))][i]
        return go([remote(buf.at[512:768, lanes], buf.at[0:256, lanes],
                          halo_send.at[i], halo_recv.at[i], nxt)])

    settle(sib_copies[1:3])
    halo_k = halo(0)
    settle(sib_copies[3:4])
    grads_rows(0, 1 - core, rates_sib[...])
    grads_sum(0)
    prim0 = prim_first(0)

    settle(py)
    part = pj.at[z, pl.ds(aligned(x, 64), 64), lanes_a]
    px = go([
        same(part, px_send.at[d - 1], px_recv.at[d - 1], along(x, 4, 8, d)) for d in (1, 2, 3)
    ])
    settle(bz)
    part = pj.at[:, place, lanes_b]
    by = go([
        same(part, by_send.at[d - 1], by_recv.at[d - 1], along(y, 4, 2, d)) for d in (1, 2, 3)
    ])
    grads_rows(1, 1 - core, rates_sib[...])
    grads_sum(1)
    settle(px)
    pz0 = pz(0, 0, 0)
    prim0 = prim_second(0, prim0)
    prim1 = prim_first(1)
    for j in range(2):
        for m in range(3):
            zacc[j, 32 * m:32 * m + 32, :] = wb[j, m, own_block, :].astype(F32)
        pack(j, wpk)
    locals_[3].wait()
    settle(sib_copies[4:5])
    attend(0, 1)
    prim_last(0, prim0)
    sec0 = sec_sends(0)
    settle(pz0)
    pz1 = pz(1, 7, 1)
    prim1 = prim_second(1, prim1)
    sec_last(0, sec0)
    z0 = z_sends(0)
    attend(1, 1)
    prim_last(1, prim1)
    sec1 = sec_sends(1)
    ag0 = renorm(0, z0)
    halo_k += halo(1)
    halo_v = halo(2)
    settle(by)
    bx0 = bx(0, [(0, 0, x_right), (0, 1, x_left), (0, 1, x_right), (0, 0, x_left)])
    sec_last(1, sec1)
    z1 = z_sends(1)
    unpack(0, ag0)
    ags0 = agsec_sends(0)
    ag1 = renorm(1, z1)
    settle(ags0)
    agp0 = agp_first(0)
    halo_v += halo(3)
    settle(pz1)
    pz2 = pz(2, 6, 2)
    unpack(1, ag1)
    ags1 = agsec_sends(1)
    agp0 = agp_second(0, agp0)
    settle(ags1)
    agp1 = agp_first(1)
    settle(bx0)
    bx1 = bx(1, [(3, 0, x_right), (1, 1, x_left)])
    settle(pz2)
    pz3 = pz(3, 5, 3, 0, 128, 128)
    settle(halo_k)
    settle(halo_v[:1])
    attend(0, 0)
    settle(halo_v[1:])
    attend(1, 0)
    agp1 = agp_second(1, agp1)
    settle(agp0)
    forward(0)
    settle(pz3)
    settle(bx1)

    their_rows = aligned(1 - core, TOK)

    def partial(rows, j, n):
        return mm_nt(comb[pl.ds(rows, TOK), j * HD:(j + 1) * HD],
                     jnp.concatenate([pj[2 * n, :, j * HD:(j + 1) * HD],
                                      pj[2 * n + 1, :, j * HD:(j + 1) * HD]], axis=0))

    for n in range(4):
        acc[0, n] = partial(their_rows, 0, n)
        acc[1, n] = partial(my_rows, 0, n)
    settle(agp1)
    forward(1)
    outs = []
    for n in range(4):
        osend[n] = (acc[0, n] + partial(their_rows, 1, n)).astype(BF16)
        outs += go([remote(osend.at[n], orecv.at[n], os_send.at[n], os_recv.at[n], sib)])
    for n in range(4):
        total = acc[1, n] + partial(my_rows, 1, n)
        outs[n].wait_recv()
        out_ref[:, n * 512:(n + 1) * 512] = (total + orecv[n].astype(F32)).astype(BF16)
    for copy in pending:
        copy.wait_send()


def body(queries, key_rows, value_rows, token_rates, fast_weights, out_gain, proj_weight):
    anywhere = pl.BlockSpec(memory_space=pl.ANY)
    vmem = pl.BlockSpec(memory_space=pltpu.VMEM)
    sem = pltpu.SemaphoreType.DMA
    scratch = [
        pltpu.VMEM((512, 1024), BF16),
        pltpu.VMEM((768, 1024), BF16),
        pltpu.VMEM((768, 1024), BF16),
        pltpu.VMEM((2, 3, 512, 512), BF16),
        pltpu.VMEM((8, 128), F32),
        pltpu.VMEM((8, 128), F32),
        pltpu.VMEM((16, 1024), BF16),
        pltpu.VMEM((16, 1024), BF16),
        pltpu.VMEM((8, 256, 1024), BF16),
        pltpu.VMEM((256, 512), F32),
        pltpu.VMEM((256, 512), F32),
        pltpu.VMEM((256, 512), F32),
        pltpu.VMEM((2, 512, 512), BF16),
        pltpu.VMEM((2, 512, 512), BF16),
        pltpu.VMEM((2, 512, 512), BF16),
        pltpu.VMEM((2, 512, 512), BF16),
        pltpu.VMEM((6, 512, 512), BF16),
        pltpu.VMEM((6, 64, 512), BF16),
        pltpu.VMEM((6, 64, 512), BF16),
        pltpu.VMEM((6, 128, 512), BF16),
        pltpu.VMEM((6, 128, 512), BF16),
        pltpu.VMEM((6, 128, 512), BF16),
        pltpu.VMEM((3, 6, 32, 512), BF16),
        pltpu.VMEM((2, 96, 512), F32),
        pltpu.VMEM((2, 8, 16, 384), BF16),
        pltpu.VMEM((2, 8, 16, 384), BF16),
        pltpu.VMEM((2, 7, 16, 384), BF16),
        pltpu.VMEM((2, 8, 16, 384), BF16),
        pltpu.VMEM((6, 512, 512), BF16),
        pltpu.VMEM((512, 1024), F32),
        pltpu.VMEM((512, 1024), BF16),
        pltpu.VMEM((2, 4, 256, 512), F32),
        pltpu.VMEM((4, 256, 512), BF16),
        pltpu.VMEM((4, 256, 512), BF16),
        sem((4,)),
        sem((5,)), sem((5,)),
        sem((12,)), sem((12,)),
        sem((6,)), sem((6,)),
        sem((14,)), sem((14,)),
        sem((14,)), sem((14,)),
        sem((6,)), sem((6,)),
        sem((12,)), sem((12,)),
        sem((3,)), sem((3,)),
        sem((3,)), sem((3,)),
        sem((8,)), sem((8,)),
        sem((7,)), sem((7,)),
        sem((3,)), sem((3,)),
        sem((8,)), sem((8,)),
        sem((4,)), sem((4,)),
        sem((4,)), sem((4,)),
    ]
    return pl.pallas_call(
        kernel,
        out_shape=pltpu.VMEM((TOK, 2048), BF16),
        in_specs=[anywhere, anywhere, anywhere, vmem, anywhere, vmem, vmem],
        out_specs=vmem,
        scratch_shapes=scratch,
        compiler_params=pltpu.CompilerParams(
            collective_id=0, has_side_effects=True, vmem_limit_bytes=56 * 1024 * 1024
        ),
        cost_estimate=pl.CostEstimate(flops=12 * 10**9, bytes_accessed=10**7, transcendentals=10**6),
    )(
        queries, key_rows, value_rows, token_rates.reshape(2, 128), fast_weights, out_gain,
        proj_weight.T,
    )


def solution(mesh):
    return jax.shard_map(
        body,
        mesh=mesh,
        in_specs=(
            P("ctx", None),
            P("ctx", None),
            P("ctx", None),
            P("ctx"),
            P(),
            P(),
            P(None, "ctx"),
        ),
        out_specs=P("ctx", None),
        check_vma=False,
    )
```

```python
import functools

import jax
import jax.numpy as jnp
from jax import lax
from jax.experimental import pallas as pl
from jax.experimental.pallas import tpu as pltpu
from jax.sharding import PartitionSpec as P

HD = 512
TOK = 256
EPS = 1e-06
CUT = 896
HALF = 32
F32 = jnp.float32
BF16 = jnp.bfloat16
MESH = pl.DeviceIdType.MESH


def mm(a, b):
    return jnp.dot(a, b, preferred_element_type=F32)


def mm_nt(a, b):
    return lax.dot_general(a, b, (((1,), (1,)), ((), ())), preferred_element_type=F32)


def mm_tn(a, b):
    return lax.dot_general(a, b, (((0,), (0,)), ((), ())), preferred_element_type=F32)


def aligned(index, step):
    return pl.multiple_of(index * step, step)


def kernel(
    q_hbm, k_hbm, v_hbm, rates_ref, w_hbm, gain_ref, proj_ref, out_ref,
    qb, kb, vb, wb, rates_st, rates_sib, pst, prx, pj,
    pg, pu, hg, og, hid, gg, ug,
    gb, ra, rb, fl, fr, sec, rsec, zacc, wpk, zs, rz, agz, wn,
    att, comb, acc, osend, orecv,
    loc_sem, sib_send, sib_recv, prim_send, prim_recv, sec_send, sec_recv,
    z_send, z_recv, agz_send, agz_recv, agsec_send, agsec_recv, agp_send, agp_recv,
    py_send, py_recv, px_send, px_recv, pz_send, pz_recv,
    bz_send, bz_recv, by_send, by_recv, bx_send, bx_recv, halo_send, halo_recv,
    os_send, os_recv,
):
    me = lax.axis_index("ctx")
    core = lax.rem(me, 2)
    chip = lax.div(me, 2)
    y = lax.rem(chip, 4)
    x = lax.rem(lax.div(chip, 4), 4)
    z = lax.div(chip, 16)
    sib = me + 1 - 2 * core
    p = core * y + (1 - core) * x
    s = core * x + (1 - core) * y
    p_step = 8 - 6 * core
    s_step = 2 + 6 * core

    def along(position, size, step, by):
        return me + (lax.rem(position + by, size) - position) * step

    right = along(p, 4, p_step, 1)
    left = along(p, 4, p_step, 3)
    z_right = along(z, 8, 32, 1)
    z_left = along(z, 8, 32, 7)
    nxt = lax.rem(me + 2, 256)
    prv = lax.rem(me + 254, 256)

    def remote(src, dst, send, recv, device):
        return pltpu.make_async_remote_copy(
            src_ref=src, dst_ref=dst, send_sem=send, recv_sem=recv,
            device_id=(device,), device_id_type=MESH,
        )

    pending = []

    def go(copies):
        for copy in copies:
            copy.start()
            pending.append(copy)
        return copies

    mine = pl.ds(aligned(core, 1024), 1024)
    theirs = pl.ds(aligned(1 - core, 1024), 1024)
    my_rows = aligned(core, TOK)
    locals_ = [
        pltpu.make_async_copy(k_hbm.at[:, mine], kb.at[pl.ds(256 + my_rows, TOK), :], loc_sem.at[0]),
        pltpu.make_async_copy(w_hbm.at[pl.ds(2 * core, 2)], wb, loc_sem.at[1]),
        pltpu.make_async_copy(v_hbm.at[:, mine], vb.at[pl.ds(256 + my_rows, TOK), :], loc_sem.at[2]),
        pltpu.make_async_copy(q_hbm.at[:, mine], qb.at[pl.ds(my_rows, TOK), :], loc_sem.at[3]),
    ]
    for copy in locals_:
        copy.start()

    barrier = pltpu.get_barrier_semaphore()
    partners = [sib, nxt, prv]
    partners += [along(x, 4, 8, d) for d in (1, 2, 3)]
    partners += [along(y, 4, 2, d) for d in (1, 2, 3)]
    partners += [along(z, 8, 32, d) for d in range(1, 8)]
    for device in partners:
        pl.semaphore_signal(barrier, inc=1, device_id=(device,), device_id_type=MESH)

    rates_st[0:2, :] = rates_ref[...]
    rates_st[2:8, :] = jnp.zeros((6, 128), F32)
    shard = proj_ref[...].astype(F32)
    first_core = core == 0
    own_half = jnp.where(first_core, shard[:, :1024], shard[:, 1024:])
    sib_half = jnp.where(first_core, shard[:, 1024:], shard[:, :1024])
    pst[...] = jnp.concatenate([sib_half, sib_half], axis=0).astype(BF16)

    pl.semaphore_wait(barrier, len(partners))

    to_sib = [
        (pst, prx),
        (rates_st, rates_sib),
        (k_hbm.at[:, theirs], kb.at[pl.ds(256 + my_rows, TOK), :]),
        (v_hbm.at[:, theirs], vb.at[pl.ds(256 + my_rows, TOK), :]),
        (q_hbm.at[:, theirs], qb.at[pl.ds(my_rows, TOK), :]),
    ]
    sib_copies = go([
        remote(src, dst, sib_send.at[i], sib_recv.at[i], sib)
        for i, (src, dst) in enumerate(to_sib)
    ])

    def grads_rows(j, block, rates):
        cols = slice(j * HD, (j + 1) * HD)
        rows = aligned(block, TOK)
        keys = kb[pl.ds(256 + rows, TOK), cols]
        for i in range(2):
            rate = jnp.transpose(jnp.broadcast_to(rates[i:i + 1, :], (128, 128)))
            rate = jnp.concatenate([rate] * 4, axis=1)
            values = vb[pl.ds(256 + rows + i * 128, 128), cols].astype(F32)
            og[j, pl.ds(rows + i * 128, 128), :] = (-rate * values).astype(BF16)
        pg[...] = mm(keys, wb[j, 0])
        pu[...] = mm(keys, wb[j, 2])
        hg[...] = mm_nt(og[j, pl.ds(rows, TOK), :], wb[j, 1])

        def step(i, carry):
            part = pl.ds(aligned(i, 32), 32)
            dest = pl.ds(rows + aligned(i, 32), 32)
            gate, up, grad = pg[part, :], pu[part, :], hg[part, :]
            sig = jax.nn.sigmoid(gate)
            act = gate * sig
            hid[j, dest, :] = (act * up).astype(BF16)
            gg[j, dest, :] = (grad * up * sig * (1.0 + gate * (1.0 - sig))).astype(BF16)
            ug[j, dest, :] = (grad * act).astype(BF16)
            return carry

        lax.fori_loop(0, 8, step, 0)

    def grads_sum(j):
        def step(i, carry):
            lanes = pl.ds(pl.multiple_of(j * HD + i * 256, 256), 256)
            out = pl.ds(aligned(i, 256), 256)
            keys = kb[256:768, lanes]
            gb[3 * j, out, :] = mm_tn(keys, gg[j]).astype(BF16)
            gb[3 * j + 2, out, :] = mm_tn(keys, ug[j]).astype(BF16)
            gb[3 * j + 1, out, :] = mm_tn(hid[j, :, pl.ds(aligned(i, 256), 256)], og[j]).astype(BF16)
            return carry

        lax.fori_loop(0, 2, step, 0)

    def chunk_rows(by, part):
        start = lax.rem(p + by, 4) * 128 + part * HALF
        return pl.ds(pl.multiple_of(start, HALF), (HALF, 128 - HALF)[part])

    def prim_first(j):
        mats = pl.ds(3 * j, 3)
        moves = [
            (gb.at[mats, chunk_rows(2, 0), :], ra.at[mats], right),
            (gb.at[mats, chunk_rows(2, 1), :], rb.at[mats], left),
            (gb.at[mats, chunk_rows(1, 1), :], fl.at[mats, HALF:128, :], right),
            (gb.at[mats, chunk_rows(3, 0), :], fr.at[mats, 0:HALF, :], left),
        ]
        return go([
            remote(src, dst, prim_send.at[6 * j + i], prim_recv.at[6 * j + i], dev)
            for i, (src, dst, dev) in enumerate(moves)
        ])

    def add_into(j, rows, extra):
        for m in range(3 * j, 3 * j + 3):
            total = gb[m, rows, :].astype(F32) + extra[m].astype(F32)
            gb[m, rows, :] = total.astype(BF16)

    def prim_second(j, first):
        mats = pl.ds(3 * j, 3)
        first[0].wait_recv()
        add_into(j, chunk_rows(1, 0), ra)
        a = remote(gb.at[mats, chunk_rows(1, 0), :], fl.at[mats, 0:HALF, :],
                   prim_send.at[6 * j + 4], prim_recv.at[6 * j + 4], right)
        go([a])
        first[1].wait_recv()
        add_into(j, chunk_rows(3, 1), rb)
        b = remote(gb.at[mats, chunk_rows(3, 1), :], fr.at[mats, HALF:128, :],
                   prim_send.at[6 * j + 5], prim_recv.at[6 * j + 5], left)
        go([b])
        return [first[2], first[3], a, b]

    def prim_last(j, copies):
        for copy in copies:
            copy.wait_recv()

        def step(i, carry):
            rows = pl.ds(aligned(i, 32), 32)
            own = pl.ds(pl.multiple_of(p * 128 + i * 32, 32), 32)
            for m in range(3 * j, 3 * j + 3):
                total = gb[m, own, :].astype(F32) + fl[m, rows, :].astype(F32)
                sec[m, rows, :] = (total + fr[m, rows, :].astype(F32)).astype(BF16)
            return carry

        lax.fori_loop(0, 4, step, 0)

    def sec_sends(j):
        mats = pl.ds(3 * j, 3)
        out = []
        for d in (1, 2, 3):
            rows = pl.ds(aligned(lax.rem(s + d, 4), 32), 32)
            out.append(remote(sec.at[mats, rows, :], rsec.at[d - 1, mats],
                              sec_send.at[3 * j + d - 1], sec_recv.at[3 * j + d - 1],
                              along(s, 4, s_step, d)))
        return go(out)

    def sec_last(j, copies):
        for copy in copies:
            copy.wait_recv()
        own = pl.ds(aligned(s, 32), 32)
        for m in range(3):
            total = sec[3 * j + m, own, :].astype(F32)
            for d in range(3):
                total = total + rsec[d, 3 * j + m].astype(F32)
            zacc[j, 32 * m:32 * m + 32, :] = total

    def pack(j, out):
        for group in range(24):
            rows = zacc[j, 4 * group:4 * group + 4, :]
            tall = jnp.concatenate([rows[:, c * 128:(c + 1) * 128] for c in range(4)], axis=0)
            lanes = slice(group % 3 * 128, (group % 3 + 1) * 128)
            out[j, group // 3, :, lanes] = tall.astype(BF16)

    def z_sends(j):
        pack(j, zs)
        return go([
            remote(zs.at[j, lax.rem(z + d, 8)], rz.at[j, d - 1],
                   z_send.at[7 * j + d - 1], z_recv.at[7 * j + d - 1], along(z, 8, 32, d))
            for d in range(1, 8)
        ])

    def renorm(j, copies):
        for copy in copies:
            copy.wait_recv()

        def rms(tall):
            square = tall * tall
            square = square[0:4] + square[4:8] + square[8:12] + square[12:16]
            return jnp.sqrt(jnp.sum(square, axis=-1, keepdims=True) * (1.0 / HD) + EPS)

        for i in range(3):
            lanes = slice(i * 128, (i + 1) * 128)
            grad = zs[j, z, :, lanes].astype(F32)
            for d in range(7):
                grad = grad + rz[j, d, :, lanes].astype(F32)
            weights = wpk[j, z, :, lanes].astype(F32)
            shifted = weights - grad
            scale = rms(weights) / rms(shifted)
            agz[j, z, :, lanes] = (shifted * jnp.concatenate([scale] * 4, axis=0)).astype(BF16)
        return go([
            remote(agz.at[j, z], agz.at[j, z], agz_send.at[7 * j + d - 1], agz_recv.at[7 * j + d - 1],
                   along(z, 8, 32, d))
            for d in range(1, 8)
        ])

    own_block = pl.ds(pl.multiple_of(128 * p + 32 * s, 32), 32)

    def unpack(j, copies):
        for copy in copies:
            copy.wait_recv()
        for m in range(3):
            rows = []
            for g in range(8 * m, 8 * m + 8):
                tall = agz[j, g // 3, :, g % 3 * 128:(g % 3 + 1) * 128].astype(F32)
                rows.append(jnp.concatenate([tall[4 * c:4 * c + 4] for c in range(4)], axis=1))
            wn[3 * j + m, own_block, :] = jnp.concatenate(rows, axis=0).astype(BF16)

    def agsec_sends(j):
        part = wn.at[pl.ds(3 * j, 3), own_block, :]
        return go([
            remote(part, part, agsec_send.at[3 * j + d - 1], agsec_recv.at[3 * j + d - 1],
                   along(s, 4, s_step, d))
            for d in (1, 2, 3)
        ])

    def agp_first(j):
        mats = pl.ds(3 * j, 3)
        half_a = wn.at[mats, chunk_rows(0, 0), :]
        half_b = wn.at[mats, chunk_rows(0, 1), :]
        moves = [(half_a, right), (half_b, left), (half_b, right), (half_a, left)]
        return go([
            remote(ref, ref, agp_send.at[6 * j + i], agp_recv.at[6 * j + i], dev)
            for i, (ref, dev) in enumerate(moves)
        ])

    def agp_second(j, first):
        mats = pl.ds(3 * j, 3)
        first[0].wait_recv()
        half_a = wn.at[mats, chunk_rows(3, 0), :]
        a = remote(half_a, half_a, agp_send.at[6 * j + 4], agp_recv.at[6 * j + 4], right)
        go([a])
        first[1].wait_recv()
        half_b = wn.at[mats, chunk_rows(1, 1), :]
        b = remote(half_b, half_b, agp_send.at[6 * j + 5], agp_recv.at[6 * j + 5], left)
        go([b])
        return [first[2], first[3], a, b]

    def attend(j, block):
        cols = slice(j * HD, (j + 1) * HD)
        first = block * TOK
        pg[...] = mm_nt(qb[first:first + TOK, cols], kb[first:first + 2 * TOK, cols])

        def step(i, carry):
            part = pl.ds(aligned(i, 64), 64)
            row = lax.broadcasted_iota(jnp.int32, (64, 512), 0) + i * 64
            col = lax.broadcasted_iota(jnp.int32, (64, 512), 1)
            valid = (col > row) & (col <= row + 256)
            if block == 0:
                valid = valid & (chip * 512 + col >= 256)
            scores = jnp.where(valid, pg[part, :] * (HD ** -0.5), -1e30)
            top = jnp.max(scores, axis=-1, keepdims=True)
            expd = jnp.exp(scores - top)
            probs = expd / jnp.sum(expd, axis=-1, keepdims=True)
            gg[0, part, :] = probs.astype(BF16)
            return carry

        lax.fori_loop(0, 4, step, 0)
        att[first:first + TOK, cols] = mm(gg[0, 0:TOK, :], vb[first:first + 2 * TOK, cols])

    def forward(j):
        cols = slice(j * HD, (j + 1) * HD)
        gain = gain_ref[pl.ds(2 * core + j, 1), :]

        def block(b, carry):
            rows = aligned(b, TOK)
            queries = qb[pl.ds(rows, TOK), cols]
            pg[...] = mm(queries, wn[3 * j])
            pu[...] = mm(queries, wn[3 * j + 2])

            def act(i, inner):
                part = pl.ds(aligned(i, 64), 64)
                gate = pg[part, :]
                gg[0, part, :] = (gate * jax.nn.sigmoid(gate) * pu[part, :]).astype(BF16)
                return inner

            lax.fori_loop(0, 4, act, 0)
            hg[...] = mm(gg[0, 0:TOK, :], wn[3 * j + 1])

            def norm(i, inner):
                part = pl.ds(aligned(i, 64), 64)
                dest = pl.ds(rows + aligned(i, 64), 64)
                fast = hg[part, :]
                scale = lax.rsqrt(jnp.mean(fast * fast, axis=-1, keepdims=True) + EPS)
                comb[dest, cols] = (att[dest, cols] + fast * scale * gain).astype(BF16)
                return inner

            lax.fori_loop(0, 4, norm, 0)
            return carry

        lax.fori_loop(0, 2, block, 0)


    sib_copies[0].wait_recv()
    received = prx[...].astype(F32)[0:8]
    pair = jnp.concatenate(
        [jnp.where(first_core, own_half, received), jnp.where(first_core, received, own_half)], axis=0
    )
    lanes_a, lanes_b = slice(0, CUT), slice(CUT, 1024)
    spot = 4 * x + y
    place = pl.ds(aligned(spot, 16), 16)
    pj[z, place, :] = pair.astype(BF16)

    def same(ref, send, recv, device):
        return remote(ref, ref, send, recv, device)

    py = go([
        same(pj.at[z, place, lanes_a], py_send.at[d - 1], py_recv.at[d - 1], along(y, 4, 2, d))
        for d in (1, 2, 3)
    ])
    bz = go([
        same(pj.at[z, place, lanes_b], bz_send.at[d - 1], bz_recv.at[d - 1], along(z, 8, 32, d))
        for d in range(1, 8)
    ])

    def settle(copies):
        for copy in copies:
            copy.wait_recv()

    def pz(step, half, by_right, by_left, sides=(0, 1)):
        blocks = (lax.rem(z + by_right, 8), lax.rem(z + by_left, 8))
        rows = slice(128 * half, 128 * half + 128)
        out = []
        for side in sides:
            ref = pj.at[blocks[side], rows, lanes_a]
            i = 4 * step + 2 * half + side
            out.append(same(ref, pz_send.at[i], pz_recv.at[i], (z_right, z_left)[side]))
        return go(out)

    x_right = along(x, 4, 8, 1)
    x_left = along(x, 4, 8, 3)

    def strip(by, half):
        start = lax.rem(x + by, 4) * 64 + half * 32
        return pj.at[:, pl.ds(pl.multiple_of(start, 32), 32), lanes_b]

    def bx(step, moves):
        return go([
            same(strip(by_, half), bx_send.at[2 * step + i], bx_recv.at[2 * step + i], dev)
            for i, (by_, half, dev) in enumerate(moves)
        ])

    def halo(i):
        buf = (kb, vb)[i // 4]
        lanes = slice(i % 4 * 256, i % 4 * 256 + 256)
        return go([remote(buf.at[512:768, lanes], buf.at[0:256, lanes],
                          halo_send.at[i], halo_recv.at[i], nxt)])

    for copy in locals_[:3]:
        copy.wait()
    grads_rows(0, core, rates_ref[...])
    settle(sib_copies[1:3])
    halo_k = halo(0) + halo(1)
    settle(py)
    part = pj.at[z, pl.ds(aligned(x, 64), 64), lanes_a]
    px = go([
        same(part, px_send.at[d - 1], px_recv.at[d - 1], along(x, 4, 8, d)) for d in (1, 2, 3)
    ])
    settle(sib_copies[3:4])
    grads_rows(0, 1 - core, rates_sib[...])
    grads_sum(0)
    prim0 = prim_first(0)

    grads_rows(1, core, rates_ref[...])
    settle(px)
    pz0a = pz(0, 0, 0, 0)
    pz0b = pz(0, 1, 0, 0)
    settle(bz)
    part = pj.at[:, place, lanes_b]
    by = go([
        same(part, by_send.at[d - 1], by_recv.at[d - 1], along(y, 4, 2, d)) for d in (1, 2, 3)
    ])
    grads_rows(1, 1 - core, rates_sib[...])
    grads_sum(1)
    prim0 = prim_second(0, prim0)
    prim1 = prim_first(1)
    for j in range(2):
        for m in range(3):
            zacc[j, 32 * m:32 * m + 32, :] = wb[j, m, own_block, :].astype(F32)
        pack(j, wpk)
    locals_[3].wait()
    settle(sib_copies[4:5])
    attend(0, 1)
    prim_last(0, prim0)
    sec0 = sec_sends(0)
    halo_k += halo(2)
    settle(pz0a)
    pz1a = pz(1, 0, 7, 1)
    prim1 = prim_second(1, prim1)
    halo_k += halo(3)
    sec_last(0, sec0)
    z0 = z_sends(0)
    attend(1, 1)
    prim_last(1, prim1)
    sec1 = sec_sends(1)
    halo_v = halo(4)
    settle(by)
    bx0 = bx(0, [(0, 0, x_right), (0, 1, x_left)])
    ag0 = renorm(0, z0)
    halo_v += halo(5)
    sec_last(1, sec1)
    z1 = z_sends(1)
    halo_v += halo(6)
    unpack(0, ag0)
    ags0 = agsec_sends(0)
    bx1 = bx(1, [(0, 1, x_right), (0, 0, x_left)])
    halo_v += halo(7)
    ag1 = renorm(1, z1)
    settle(pz0b)
    pz1b = pz(1, 1, 7, 1)
    settle(pz1a)
    pz2a = pz(2, 0, 6, 2)
    settle(ags0)
    agp0 = agp_first(0)
    unpack(1, ag1)
    ags1 = agsec_sends(1)
    agp0 = agp_second(0, agp0)
    settle(ags1)
    agp1 = agp_first(1)
    settle(bx0)
    bx2 = bx(2, [(3, 0, x_right), (1, 1, x_left)])
    settle(pz1b)
    pz2b = pz(2, 1, 6, 2)
    settle(pz2a)
    pz3 = pz(3, 0, 5, 3, (0,))
    settle(halo_k)
    settle(halo_v[:2])
    attend(0, 0)
    settle(halo_v[2:])
    attend(1, 0)
    settle(pz2b)
    pz3 += pz(3, 1, 5, 3, (1,))
    agp1 = agp_second(1, agp1)
    settle(agp0)
    forward(0)
    settle(pz3)
    settle(bx1)
    settle(bx2)

    their_rows = aligned(1 - core, TOK)

    def partial(rows, j, n):
        return mm_nt(comb[pl.ds(rows, TOK), j * HD:(j + 1) * HD],
                     jnp.concatenate([pj[2 * n, :, j * HD:(j + 1) * HD],
                                      pj[2 * n + 1, :, j * HD:(j + 1) * HD]], axis=0))

    for n in range(4):
        acc[0, n] = partial(their_rows, 0, n)
        acc[1, n] = partial(my_rows, 0, n)
    settle(agp1)
    forward(1)
    outs = []
    for n in range(4):
        osend[n] = (acc[0, n] + partial(their_rows, 1, n)).astype(BF16)
        outs += go([remote(osend.at[n], orecv.at[n], os_send.at[n], os_recv.at[n], sib)])
    for n in range(4):
        total = acc[1, n] + partial(my_rows, 1, n)
        outs[n].wait_recv()
        out_ref[:, n * 512:(n + 1) * 512] = (total + orecv[n].astype(F32)).astype(BF16)
    for copy in pending:
        copy.wait_send()


def body(queries, key_rows, value_rows, token_rates, fast_weights, out_gain, proj_weight):
    anywhere = pl.BlockSpec(memory_space=pl.ANY)
    vmem = pl.BlockSpec(memory_space=pltpu.VMEM)
    sem = pltpu.SemaphoreType.DMA
    scratch = [
        pltpu.VMEM((512, 1024), BF16),
        pltpu.VMEM((768, 1024), BF16),
        pltpu.VMEM((768, 1024), BF16),
        pltpu.VMEM((2, 3, 512, 512), BF16),
        pltpu.VMEM((8, 128), F32),
        pltpu.VMEM((8, 128), F32),
        pltpu.VMEM((16, 1024), BF16),
        pltpu.VMEM((16, 1024), BF16),
        pltpu.VMEM((8, 256, 1024), BF16),
        pltpu.VMEM((256, 512), F32),
        pltpu.VMEM((256, 512), F32),
        pltpu.VMEM((256, 512), F32),
        pltpu.VMEM((2, 512, 512), BF16),
        pltpu.VMEM((2, 512, 512), BF16),
        pltpu.VMEM((2, 512, 512), BF16),
        pltpu.VMEM((2, 512, 512), BF16),
        pltpu.VMEM((6, 512, 512), BF16),
        pltpu.VMEM((6, HALF, 512), BF16),
        pltpu.VMEM((6, 128 - HALF, 512), BF16),
        pltpu.VMEM((6, 128, 512), BF16),
        pltpu.VMEM((6, 128, 512), BF16),
        pltpu.VMEM((6, 128, 512), BF16),
        pltpu.VMEM((3, 6, 32, 512), BF16),
        pltpu.VMEM((2, 96, 512), F32),
        pltpu.VMEM((2, 8, 16, 384), BF16),
        pltpu.VMEM((2, 8, 16, 384), BF16),
        pltpu.VMEM((2, 7, 16, 384), BF16),
        pltpu.VMEM((2, 8, 16, 384), BF16),
        pltpu.VMEM((6, 512, 512), BF16),
        pltpu.VMEM((512, 1024), F32),
        pltpu.VMEM((512, 1024), BF16),
        pltpu.VMEM((2, 4, 256, 512), F32),
        pltpu.VMEM((4, 256, 512), BF16),
        pltpu.VMEM((4, 256, 512), BF16),
        sem((4,)),
        sem((5,)), sem((5,)),
        sem((12,)), sem((12,)),
        sem((6,)), sem((6,)),
        sem((14,)), sem((14,)),
        sem((14,)), sem((14,)),
        sem((6,)), sem((6,)),
        sem((12,)), sem((12,)),
        sem((3,)), sem((3,)),
        sem((3,)), sem((3,)),
        sem((16,)), sem((16,)),
        sem((7,)), sem((7,)),
        sem((3,)), sem((3,)),
        sem((8,)), sem((8,)),
        sem((8,)), sem((8,)),
        sem((4,)), sem((4,)),
    ]
    return pl.pallas_call(
        kernel,
        out_shape=pltpu.VMEM((TOK, 2048), BF16),
        in_specs=[anywhere, anywhere, anywhere, vmem, anywhere, vmem, vmem],
        out_specs=vmem,
        scratch_shapes=scratch,
        compiler_params=pltpu.CompilerParams(
            collective_id=0, has_side_effects=True, vmem_limit_bytes=56 * 1024 * 1024
        ),
        cost_estimate=pl.CostEstimate(flops=12 * 10**9, bytes_accessed=10**7, transcendentals=10**6),
    )(
        queries, key_rows, value_rows, token_rates.reshape(2, 128), fast_weights, out_gain,
        proj_weight.T,
    )


def solution(mesh):
    return jax.shard_map(
        body,
        mesh=mesh,
        in_specs=(
            P("ctx", None),
            P("ctx", None),
            P("ctx", None),
            P("ctx"),
            P(),
            P(),
            P(None, "ctx"),
        ),
        out_specs=P("ctx", None),
        check_vma=False,
    )
```

```python
import functools

import jax
import jax.numpy as jnp
from jax import lax
from jax.experimental import pallas as pl
from jax.experimental.pallas import tpu as pltpu
from jax.sharding import PartitionSpec as P

HD = 512
TOK = 256
EPS = 1e-06
CUT = 896
HALF = 32
F32 = jnp.float32
BF16 = jnp.bfloat16
MESH = pl.DeviceIdType.MESH


def mm(a, b):
    return jnp.dot(a, b, preferred_element_type=F32)


def mm_nt(a, b):
    return lax.dot_general(a, b, (((1,), (1,)), ((), ())), preferred_element_type=F32)


def mm_tn(a, b):
    return lax.dot_general(a, b, (((0,), (0,)), ((), ())), preferred_element_type=F32)


def aligned(index, step):
    return pl.multiple_of(index * step, step)


def kernel(
    q_hbm, k_hbm, v_hbm, rates_ref, w_hbm, gain_ref, proj_ref, out_ref,
    qb, kb, vb, wb, rates_st, rates_sib, pst, prx, pj,
    pg, pu, hg, og, hid, gg, ug,
    gb, ra, rb, fl, fr, sec, rsec, zacc, wpk, zs, rz, agz, wn,
    att, comb, acc, osend, orecv,
    loc_sem, sib_send, sib_recv, prim_send, prim_recv, sec_send, sec_recv,
    z_send, z_recv, agz_send, agz_recv, agsec_send, agsec_recv, agp_send, agp_recv,
    py_send, py_recv, px_send, px_recv, pz_send, pz_recv,
    bz_send, bz_recv, by_send, by_recv, bx_send, bx_recv, halo_send, halo_recv,
    os_send, os_recv,
):
    me = lax.axis_index("ctx")
    core = lax.rem(me, 2)
    chip = lax.div(me, 2)
    y = lax.rem(chip, 4)
    x = lax.rem(lax.div(chip, 4), 4)
    z = lax.div(chip, 16)
    sib = me + 1 - 2 * core
    p = core * y + (1 - core) * x
    s = core * x + (1 - core) * y
    p_step = 8 - 6 * core
    s_step = 2 + 6 * core

    def along(position, size, step, by):
        return me + (lax.rem(position + by, size) - position) * step

    right = along(p, 4, p_step, 1)
    left = along(p, 4, p_step, 3)
    z_right = along(z, 8, 32, 1)
    z_left = along(z, 8, 32, 7)
    nxt = lax.rem(me + 2, 256)
    prv = lax.rem(me + 254, 256)

    def remote(src, dst, send, recv, device):
        return pltpu.make_async_remote_copy(
            src_ref=src, dst_ref=dst, send_sem=send, recv_sem=recv,
            device_id=(device,), device_id_type=MESH,
        )

    pending = []

    def go(copies):
        for copy in copies:
            copy.start()
            pending.append(copy)
        return copies

    mine = pl.ds(aligned(core, 1024), 1024)
    theirs = pl.ds(aligned(1 - core, 1024), 1024)
    my_rows = aligned(core, TOK)
    locals_ = [
        pltpu.make_async_copy(k_hbm.at[:, mine], kb.at[pl.ds(256 + my_rows, TOK), :], loc_sem.at[0]),
        pltpu.make_async_copy(w_hbm.at[pl.ds(2 * core, 2)], wb, loc_sem.at[1]),
        pltpu.make_async_copy(v_hbm.at[:, mine], vb.at[pl.ds(256 + my_rows, TOK), :], loc_sem.at[2]),
        pltpu.make_async_copy(q_hbm.at[:, mine], qb.at[pl.ds(my_rows, TOK), :], loc_sem.at[3]),
    ]
    for copy in locals_:
        copy.start()

    barrier = pltpu.get_barrier_semaphore()
    partners = [sib, nxt, prv]
    partners += [along(x, 4, 8, d) for d in (1, 2, 3)]
    partners += [along(y, 4, 2, d) for d in (1, 2, 3)]
    partners += [along(z, 8, 32, d) for d in range(1, 8)]
    for device in partners:
        pl.semaphore_signal(barrier, inc=1, device_id=(device,), device_id_type=MESH)

    rates_st[0:2, :] = rates_ref[...]
    rates_st[2:8, :] = jnp.zeros((6, 128), F32)
    shard = proj_ref[...].astype(F32)
    first_core = core == 0
    own_half = jnp.where(first_core, shard[:, :1024], shard[:, 1024:])
    sib_half = jnp.where(first_core, shard[:, 1024:], shard[:, :1024])
    pst[...] = jnp.concatenate([sib_half, sib_half], axis=0).astype(BF16)

    pl.semaphore_wait(barrier, len(partners))

    to_sib = [
        (pst, prx),
        (rates_st, rates_sib),
        (k_hbm.at[:, theirs], kb.at[pl.ds(256 + my_rows, TOK), :]),
        (v_hbm.at[:, theirs], vb.at[pl.ds(256 + my_rows, TOK), :]),
        (q_hbm.at[:, theirs], qb.at[pl.ds(my_rows, TOK), :]),
    ]
    sib_copies = go([
        remote(src, dst, sib_send.at[i], sib_recv.at[i], sib)
        for i, (src, dst) in enumerate(to_sib)
    ])

    def grads_rows(j, block, rates):
        cols = slice(j * HD, (j + 1) * HD)
        rows = aligned(block, TOK)
        keys = kb[pl.ds(256 + rows, TOK), cols]
        for i in range(2):
            rate = jnp.transpose(jnp.broadcast_to(rates[i:i + 1, :], (128, 128)))
            rate = jnp.concatenate([rate] * 4, axis=1)
            values = vb[pl.ds(256 + rows + i * 128, 128), cols].astype(F32)
            og[j, pl.ds(rows + i * 128, 128), :] = (-rate * values).astype(BF16)
        pg[...] = mm(keys, wb[j, 0])
        pu[...] = mm(keys, wb[j, 2])
        hg[...] = mm_nt(og[j, pl.ds(rows, TOK), :], wb[j, 1])

        def step(i, carry):
            part = pl.ds(aligned(i, 32), 32)
            dest = pl.ds(rows + aligned(i, 32), 32)
            gate, up, grad = pg[part, :], pu[part, :], hg[part, :]
            sig = jax.nn.sigmoid(gate)
            act = gate * sig
            hid[j, dest, :] = (act * up).astype(BF16)
            gg[j, dest, :] = (grad * up * sig * (1.0 + gate * (1.0 - sig))).astype(BF16)
            ug[j, dest, :] = (grad * act).astype(BF16)
            return carry

        lax.fori_loop(0, 8, step, 0)

    def grads_sum(j):
        def step(i, carry):
            lanes = pl.ds(pl.multiple_of(j * HD + i * 256, 256), 256)
            out = pl.ds(aligned(i, 256), 256)
            keys = kb[256:768, lanes]
            gb[3 * j, out, :] = mm_tn(keys, gg[j]).astype(BF16)
            gb[3 * j + 2, out, :] = mm_tn(keys, ug[j]).astype(BF16)
            gb[3 * j + 1, out, :] = mm_tn(hid[j, :, pl.ds(aligned(i, 256), 256)], og[j]).astype(BF16)
            return carry

        lax.fori_loop(0, 2, step, 0)

    def chunk_rows(by, part):
        start = lax.rem(p + by, 4) * 128 + part * HALF
        return pl.ds(pl.multiple_of(start, HALF), (HALF, 128 - HALF)[part])

    def prim_first(j):
        mats = pl.ds(3 * j, 3)
        moves = [
            (gb.at[mats, chunk_rows(2, 0), :], ra.at[mats], right),
            (gb.at[mats, chunk_rows(2, 1), :], rb.at[mats], left),
            (gb.at[mats, chunk_rows(1, 1), :], fl.at[mats, HALF:128, :], right),
            (gb.at[mats, chunk_rows(3, 0), :], fr.at[mats, 0:HALF, :], left),
        ]
        return go([
            remote(src, dst, prim_send.at[6 * j + i], prim_recv.at[6 * j + i], dev)
            for i, (src, dst, dev) in enumerate(moves)
        ])

    def add_into(j, rows, extra):
        for m in range(3 * j, 3 * j + 3):
            total = gb[m, rows, :].astype(F32) + extra[m].astype(F32)
            gb[m, rows, :] = total.astype(BF16)

    def prim_second(j, first):
        mats = pl.ds(3 * j, 3)
        first[0].wait_recv()
        add_into(j, chunk_rows(1, 0), ra)
        a = remote(gb.at[mats, chunk_rows(1, 0), :], fl.at[mats, 0:HALF, :],
                   prim_send.at[6 * j + 4], prim_recv.at[6 * j + 4], right)
        go([a])
        first[1].wait_recv()
        add_into(j, chunk_rows(3, 1), rb)
        b = remote(gb.at[mats, chunk_rows(3, 1), :], fr.at[mats, HALF:128, :],
                   prim_send.at[6 * j + 5], prim_recv.at[6 * j + 5], left)
        go([b])
        return [first[2], first[3], a, b]

    def prim_last(j, copies):
        for copy in copies:
            copy.wait_recv()

        def step(i, carry):
            rows = pl.ds(aligned(i, 32), 32)
            own = pl.ds(pl.multiple_of(p * 128 + i * 32, 32), 32)
            for m in range(3 * j, 3 * j + 3):
                total = gb[m, own, :].astype(F32) + fl[m, rows, :].astype(F32)
                sec[m, rows, :] = (total + fr[m, rows, :].astype(F32)).astype(BF16)
            return carry

        lax.fori_loop(0, 4, step, 0)

    def sec_sends(j):
        mats = pl.ds(3 * j, 3)
        out = []
        for d in (1, 2, 3):
            rows = pl.ds(aligned(lax.rem(s + d, 4), 32), 32)
            out.append(remote(sec.at[mats, rows, :], rsec.at[d - 1, mats],
                              sec_send.at[3 * j + d - 1], sec_recv.at[3 * j + d - 1],
                              along(s, 4, s_step, d)))
        return go(out)

    def sec_last(j, copies):
        for copy in copies:
            copy.wait_recv()
        own = pl.ds(aligned(s, 32), 32)
        for m in range(3):
            total = sec[3 * j + m, own, :].astype(F32)
            for d in range(3):
                total = total + rsec[d, 3 * j + m].astype(F32)
            zacc[j, 32 * m:32 * m + 32, :] = total

    def pack(j, out):
        for group in range(24):
            rows = zacc[j, 4 * group:4 * group + 4, :]
            tall = jnp.concatenate([rows[:, c * 128:(c + 1) * 128] for c in range(4)], axis=0)
            lanes = slice(group % 3 * 128, (group % 3 + 1) * 128)
            out[j, group // 3, :, lanes] = tall.astype(BF16)

    def z_sends(j):
        pack(j, zs)
        return go([
            remote(zs.at[j, lax.rem(z + d, 8)], rz.at[j, d - 1],
                   z_send.at[7 * j + d - 1], z_recv.at[7 * j + d - 1], along(z, 8, 32, d))
            for d in range(1, 8)
        ])

    def renorm(j, copies):
        for copy in copies:
            copy.wait_recv()

        def rms(tall):
            square = tall * tall
            square = square[0:4] + square[4:8] + square[8:12] + square[12:16]
            return jnp.sqrt(jnp.sum(square, axis=-1, keepdims=True) * (1.0 / HD) + EPS)

        for i in range(3):
            lanes = slice(i * 128, (i + 1) * 128)
            grad = zs[j, z, :, lanes].astype(F32)
            for d in range(7):
                grad = grad + rz[j, d, :, lanes].astype(F32)
            weights = wpk[j, z, :, lanes].astype(F32)
            shifted = weights - grad
            scale = rms(weights) / rms(shifted)
            agz[j, z, :, lanes] = (shifted * jnp.concatenate([scale] * 4, axis=0)).astype(BF16)
        return go([
            remote(agz.at[j, z], agz.at[j, z], agz_send.at[7 * j + d - 1], agz_recv.at[7 * j + d - 1],
                   along(z, 8, 32, d))
            for d in range(1, 8)
        ])

    own_block = pl.ds(pl.multiple_of(128 * p + 32 * s, 32), 32)

    def unpack(j, copies):
        for copy in copies:
            copy.wait_recv()
        for m in range(3):
            rows = []
            for g in range(8 * m, 8 * m + 8):
                tall = agz[j, g // 3, :, g % 3 * 128:(g % 3 + 1) * 128].astype(F32)
                rows.append(jnp.concatenate([tall[4 * c:4 * c + 4] for c in range(4)], axis=1))
            wn[3 * j + m, own_block, :] = jnp.concatenate(rows, axis=0).astype(BF16)

    def agsec_sends(j):
        part = wn.at[pl.ds(3 * j, 3), own_block, :]
        return go([
            remote(part, part, agsec_send.at[3 * j + d - 1], agsec_recv.at[3 * j + d - 1],
                   along(s, 4, s_step, d))
            for d in (1, 2, 3)
        ])

    def agp_first(j):
        mats = pl.ds(3 * j, 3)
        half_a = wn.at[mats, chunk_rows(0, 0), :]
        half_b = wn.at[mats, chunk_rows(0, 1), :]
        moves = [(half_a, right), (half_b, left), (half_b, right), (half_a, left)]
        return go([
            remote(ref, ref, agp_send.at[6 * j + i], agp_recv.at[6 * j + i], dev)
            for i, (ref, dev) in enumerate(moves)
        ])

    def agp_second(j, first):
        mats = pl.ds(3 * j, 3)
        first[0].wait_recv()
        half_a = wn.at[mats, chunk_rows(3, 0), :]
        a = remote(half_a, half_a, agp_send.at[6 * j + 4], agp_recv.at[6 * j + 4], right)
        go([a])
        first[1].wait_recv()
        half_b = wn.at[mats, chunk_rows(1, 1), :]
        b = remote(half_b, half_b, agp_send.at[6 * j + 5], agp_recv.at[6 * j + 5], left)
        go([b])
        return [first[2], first[3], a, b]

    def attend(j, block):
        cols = slice(j * HD, (j + 1) * HD)
        first = block * TOK
        pg[...] = mm_nt(qb[first:first + TOK, cols], kb[first:first + 2 * TOK, cols])

        def step(i, carry):
            part = pl.ds(aligned(i, 64), 64)
            row = lax.broadcasted_iota(jnp.int32, (64, 512), 0) + i * 64
            col = lax.broadcasted_iota(jnp.int32, (64, 512), 1)
            valid = (col > row) & (col <= row + 256)
            if block == 0:
                valid = valid & (chip * 512 + col >= 256)
            scores = jnp.where(valid, pg[part, :] * (HD ** -0.5), -1e30)
            top = jnp.max(scores, axis=-1, keepdims=True)
            expd = jnp.exp(scores - top)
            probs = expd / jnp.sum(expd, axis=-1, keepdims=True)
            gg[0, part, :] = probs.astype(BF16)
            return carry

        lax.fori_loop(0, 4, step, 0)
        att[first:first + TOK, cols] = mm(gg[0, 0:TOK, :], vb[first:first + 2 * TOK, cols])

    def forward(j):
        cols = slice(j * HD, (j + 1) * HD)
        gain = gain_ref[pl.ds(2 * core + j, 1), :]

        def block(b, carry):
            rows = aligned(b, TOK)
            queries = qb[pl.ds(rows, TOK), cols]
            pg[...] = mm(queries, wn[3 * j])
            pu[...] = mm(queries, wn[3 * j + 2])

            def act(i, inner):
                part = pl.ds(aligned(i, 64), 64)
                gate = pg[part, :]
                gg[0, part, :] = (gate * jax.nn.sigmoid(gate) * pu[part, :]).astype(BF16)
                return inner

            lax.fori_loop(0, 4, act, 0)
            hg[...] = mm(gg[0, 0:TOK, :], wn[3 * j + 1])

            def norm(i, inner):
                part = pl.ds(aligned(i, 64), 64)
                dest = pl.ds(rows + aligned(i, 64), 64)
                fast = hg[part, :]
                scale = lax.rsqrt(jnp.mean(fast * fast, axis=-1, keepdims=True) + EPS)
                comb[dest, cols] = (att[dest, cols] + fast * scale * gain).astype(BF16)
                return inner

            lax.fori_loop(0, 4, norm, 0)
            return carry

        lax.fori_loop(0, 2, block, 0)


    sib_copies[0].wait_recv()
    received = prx[...].astype(F32)[0:8]
    pair = jnp.concatenate(
        [jnp.where(first_core, own_half, received), jnp.where(first_core, received, own_half)], axis=0
    )
    lanes_a, lanes_b = slice(0, CUT), slice(CUT, 1024)
    spot = 4 * x + y
    place = pl.ds(aligned(spot, 16), 16)
    pj[z, place, :] = pair.astype(BF16)

    def same(ref, send, recv, device):
        return remote(ref, ref, send, recv, device)

    py = go([
        same(pj.at[z, place, lanes_a], py_send.at[d - 1], py_recv.at[d - 1], along(y, 4, 2, d))
        for d in (1, 2, 3)
    ])
    bz = go([
        same(pj.at[z, place, lanes_b], bz_send.at[d - 1], bz_recv.at[d - 1], along(z, 8, 32, d))
        for d in range(1, 8)
    ])

    def settle(copies):
        for copy in copies:
            copy.wait_recv()

    def pz(step, half, by_right, by_left, sides=(0, 1)):
        blocks = (lax.rem(z + by_right, 8), lax.rem(z + by_left, 8))
        rows = slice(128 * half, 128 * half + 128)
        out = []
        for side in sides:
            ref = pj.at[blocks[side], rows, lanes_a]
            i = 4 * step + 2 * half + side
            out.append(same(ref, pz_send.at[i], pz_recv.at[i], (z_right, z_left)[side]))
        return go(out)

    x_right = along(x, 4, 8, 1)
    x_left = along(x, 4, 8, 3)

    def strip(by, half):
        start = lax.rem(x + by, 4) * 64 + half * 32
        return pj.at[:, pl.ds(pl.multiple_of(start, 32), 32), lanes_b]

    def bx(step, moves):
        return go([
            same(strip(by_, half), bx_send.at[2 * step + i], bx_recv.at[2 * step + i], dev)
            for i, (by_, half, dev) in enumerate(moves)
        ])

    def halo(i):
        buf = (kb, vb)[i // 4]
        lanes = slice(i % 4 * 256, i % 4 * 256 + 256)
        return go([remote(buf.at[512:768, lanes], buf.at[0:256, lanes],
                          halo_send.at[i], halo_recv.at[i], nxt)])

    for copy in locals_[:3]:
        copy.wait()
    settle(sib_copies[2:3])
    halo_all = halo(0) + halo(1)
    grads_rows(0, core, rates_ref[...])
    settle(sib_copies[1:2])
    settle(py)
    part = pj.at[z, pl.ds(aligned(x, 64), 64), lanes_a]
    px = go([
        same(part, px_send.at[d - 1], px_recv.at[d - 1], along(x, 4, 8, d)) for d in (1, 2, 3)
    ])
    settle(sib_copies[3:4])
    grads_rows(0, 1 - core, rates_sib[...])
    grads_sum(0)
    prim0 = prim_first(0)

    grads_rows(1, core, rates_ref[...])
    settle(px)
    pz0a = pz(0, 0, 0, 0)
    pz0b = pz(0, 1, 0, 0)
    settle(bz)
    part = pj.at[:, place, lanes_b]
    by = go([
        same(part, by_send.at[d - 1], by_recv.at[d - 1], along(y, 4, 2, d)) for d in (1, 2, 3)
    ])
    grads_rows(1, 1 - core, rates_sib[...])
    grads_sum(1)
    prim0 = prim_second(0, prim0)
    prim1 = prim_first(1)
    for j in range(2):
        for m in range(3):
            zacc[j, 32 * m:32 * m + 32, :] = wb[j, m, own_block, :].astype(F32)
        pack(j, wpk)
    locals_[3].wait()
    settle(sib_copies[4:5])
    attend(0, 1)
    prim_last(0, prim0)
    sec0 = sec_sends(0)
    halo_all += halo(2)
    settle(pz0a)
    pz1a = pz(1, 0, 7, 1)
    prim1 = prim_second(1, prim1)
    halo_all += halo(3)
    sec_last(0, sec0)
    z0 = z_sends(0)
    attend(1, 1)
    prim_last(1, prim1)
    sec1 = sec_sends(1)
    halo_all += halo(4)
    halo_all += halo(5)
    settle(by)
    bx0 = bx(0, [(0, 0, x_right), (0, 1, x_left)])
    ag0 = renorm(0, z0)
    halo_all += halo(6)
    sec_last(1, sec1)
    z1 = z_sends(1)
    halo_all += halo(7)
    unpack(0, ag0)
    ags0 = agsec_sends(0)
    bx1 = bx(1, [(0, 1, x_right), (0, 0, x_left)])
    ag1 = renorm(1, z1)
    settle(pz0b)
    pz1b = pz(1, 1, 7, 1)
    settle(pz1a)
    pz2a = pz(2, 0, 6, 2)
    settle(ags0)
    agp0 = agp_first(0)
    unpack(1, ag1)
    ags1 = agsec_sends(1)
    agp0 = agp_second(0, agp0)
    settle(ags1)
    agp1 = agp_first(1)
    settle(bx0)
    bx2 = bx(2, [(3, 0, x_right), (1, 1, x_left)])
    settle(pz1b)
    pz2b = pz(2, 1, 6, 2)
    settle(pz2a)
    pz3 = pz(3, 0, 5, 3, (0,))
    settle([halo_all[i] for i in (0, 1, 2, 3, 4, 5)])
    attend(0, 0)
    settle(halo_all[6:])
    attend(1, 0)
    settle(pz2b)
    pz3 += pz(3, 1, 5, 3, (1,))
    agp1 = agp_second(1, agp1)
    settle(agp0)
    forward(0)
    settle(pz3)
    settle(bx1)
    settle(bx2)

    their_rows = aligned(1 - core, TOK)

    def partial(rows, j, n):
        return mm_nt(comb[pl.ds(rows, TOK), j * HD:(j + 1) * HD],
                     jnp.concatenate([pj[2 * n, :, j * HD:(j + 1) * HD],
                                      pj[2 * n + 1, :, j * HD:(j + 1) * HD]], axis=0))

    for n in range(4):
        acc[0, n] = partial(their_rows, 0, n)
        acc[1, n] = partial(my_rows, 0, n)
    settle(agp1)
    forward(1)
    outs = []
    for n in range(4):
        osend[n] = (acc[0, n] + partial(their_rows, 1, n)).astype(BF16)
        outs += go([remote(osend.at[n], orecv.at[n], os_send.at[n], os_recv.at[n], sib)])
    for n in range(4):
        total = acc[1, n] + partial(my_rows, 1, n)
        outs[n].wait_recv()
        out_ref[:, n * 512:(n + 1) * 512] = (total + orecv[n].astype(F32)).astype(BF16)
    for copy in pending:
        copy.wait_send()


def body(queries, key_rows, value_rows, token_rates, fast_weights, out_gain, proj_weight):
    anywhere = pl.BlockSpec(memory_space=pl.ANY)
    vmem = pl.BlockSpec(memory_space=pltpu.VMEM)
    sem = pltpu.SemaphoreType.DMA
    scratch = [
        pltpu.VMEM((512, 1024), BF16),
        pltpu.VMEM((768, 1024), BF16),
        pltpu.VMEM((768, 1024), BF16),
        pltpu.VMEM((2, 3, 512, 512), BF16),
        pltpu.VMEM((8, 128), F32),
        pltpu.VMEM((8, 128), F32),
        pltpu.VMEM((16, 1024), BF16),
        pltpu.VMEM((16, 1024), BF16),
        pltpu.VMEM((8, 256, 1024), BF16),
        pltpu.VMEM((256, 512), F32),
        pltpu.VMEM((256, 512), F32),
        pltpu.VMEM((256, 512), F32),
        pltpu.VMEM((2, 512, 512), BF16),
        pltpu.VMEM((2, 512, 512), BF16),
        pltpu.VMEM((2, 512, 512), BF16),
        pltpu.VMEM((2, 512, 512), BF16),
        pltpu.VMEM((6, 512, 512), BF16),
        pltpu.VMEM((6, HALF, 512), BF16),
        pltpu.VMEM((6, 128 - HALF, 512), BF16),
        pltpu.VMEM((6, 128, 512), BF16),
        pltpu.VMEM((6, 128, 512), BF16),
        pltpu.VMEM((6, 128, 512), BF16),
        pltpu.VMEM((3, 6, 32, 512), BF16),
        pltpu.VMEM((2, 96, 512), F32),
        pltpu.VMEM((2, 8, 16, 384), BF16),
        pltpu.VMEM((2, 8, 16, 384), BF16),
        pltpu.VMEM((2, 7, 16, 384), BF16),
        pltpu.VMEM((2, 8, 16, 384), BF16),
        pltpu.VMEM((6, 512, 512), BF16),
        pltpu.VMEM((512, 1024), F32),
        pltpu.VMEM((512, 1024), BF16),
        pltpu.VMEM((2, 4, 256, 512), F32),
        pltpu.VMEM((4, 256, 512), BF16),
        pltpu.VMEM((4, 256, 512), BF16),
        sem((4,)),
        sem((5,)), sem((5,)),
        sem((12,)), sem((12,)),
        sem((6,)), sem((6,)),
        sem((14,)), sem((14,)),
        sem((14,)), sem((14,)),
        sem((6,)), sem((6,)),
        sem((12,)), sem((12,)),
        sem((3,)), sem((3,)),
        sem((3,)), sem((3,)),
        sem((16,)), sem((16,)),
        sem((7,)), sem((7,)),
        sem((3,)), sem((3,)),
        sem((8,)), sem((8,)),
        sem((8,)), sem((8,)),
        sem((4,)), sem((4,)),
    ]
    return pl.pallas_call(
        kernel,
        out_shape=pltpu.VMEM((TOK, 2048), BF16),
        in_specs=[anywhere, anywhere, anywhere, vmem, anywhere, vmem, vmem],
        out_specs=vmem,
        scratch_shapes=scratch,
        compiler_params=pltpu.CompilerParams(
            collective_id=0, has_side_effects=True, vmem_limit_bytes=56 * 1024 * 1024
        ),
        cost_estimate=pl.CostEstimate(flops=12 * 10**9, bytes_accessed=10**7, transcendentals=10**6),
    )(
        queries, key_rows, value_rows, token_rates.reshape(2, 128), fast_weights, out_gain,
        proj_weight.T,
    )


def solution(mesh):
    return jax.shard_map(
        body,
        mesh=mesh,
        in_specs=(
            P("ctx", None),
            P("ctx", None),
            P("ctx", None),
            P("ctx"),
            P(),
            P(),
            P(None, "ctx"),
        ),
        out_specs=P("ctx", None),
        check_vma=False,
    )
```
